256 devices in a mesh: blk: 8 (over x_hi, y), grp: 32 (over x_lo, z, core).
Axes of the slice: x: 4 (x_hi: 2, x_lo: 2; x = x_hi * 2 + x_lo), y: 4, z: 8, core: 2. Of those that a mesh axis runs over, the one named last changes fastest.
Arguments:
- spot_features: bfloat16 [64, 49152], P(None, ('blk', 'grp')), may hold values from -32 to 32
- spot_factors: bfloat16 [34, 49152], P(None, ('blk', 'grp')), may hold values from -52 to 52
- spot_log_mass: float32 [49152], P(('blk', 'grp')), may hold values from -1 to 1
- cell_features: bfloat16 [64, 49152], P(None, ('blk', 'grp')), may hold values from -2 to 2
- cell_factors: bfloat16 [34, 49152], P(None, ('blk', 'grp')), may hold values from -1 to 1
- cell_log_mass: float32 [49152], P(('blk', 'grp')), may hold values from -1 to 1
- cell_potential: float32 [49152], P(('blk', 'grp')), may hold values from -50 to 1
Outputs:
- spot_potential: float32 [49152], P(('blk', 'grp'))
- cell_update: float32 [49152], P(('blk', 'grp'))
The draws below stay inside these ranges and needn't reach their ends.
All inputs are finite; a program needn't handle non-finite values.
Results may differ from the reference program's by a relative error of at most 0.0003.
Values may be sent and summed in bfloat16 or wider, within the bound.
A program may use at most 128 MiB of HBM per device.

```python
import math
import jax
import jax.numpy as jnp
from jax import lax

F = 64
R = 34
N_SPOTS = 49152
N_CELLS = 49152


aligned_count = 16


def drawn_plan(key):
    key = jax.random.fold_in(key, 7)
    spot_key, cell_key, sign_key, depth_key, gap_key = jax.random.split(key, 5)
    spot_order = jax.random.permutation(spot_key, N_SPOTS)[:2 * aligned_count]
    cell_order = jax.random.permutation(cell_key, N_CELLS)[:2 * aligned_count]
    sign_table = (2 * jax.random.randint(sign_key, (aligned_count, R), 0, 2) - 1).astype(jnp.float32)
    depth_level = jax.random.uniform(depth_key, (aligned_count,), jnp.float32, 12.0, 50.0)
    gap_level = jax.random.uniform(gap_key, (aligned_count,), jnp.float32, 0.25, 0.75)
    return (spot_order, cell_order[:aligned_count], cell_order[aligned_count:], sign_table, depth_level, gap_level)


def random_signs(key, shape):
    return (2 * jax.random.randint(key, shape, 0, 2) - 1).astype(jnp.float32)


def draw_spot_features(key, part):
    key = jax.random.fold_in(key, 11)
    noise_key = jax.random.fold_in(key, 0)
    values = jax.random.normal(noise_key, (F, N_SPOTS), jnp.float32)
    return jnp.clip(values, -5.0, 5.0).astype(jnp.bfloat16)


def draw_spot_factors(key, part):
    spot_order, first_cells, second_cells, sign_table, depth_level, gap_level = drawn_plan(key)
    key = jax.random.fold_in(key, 37)
    values = jnp.clip(jax.random.normal(key, (R, N_SPOTS), jnp.float32), -5.0, 5.0)
    strength = 0.9 * depth_level + 6.0
    aligned_rows = -strength[:, None] * sign_table
    aligned_rows = jnp.concatenate([aligned_rows, aligned_rows], axis=0)
    values = values.at[:, spot_order].set(jnp.transpose(aligned_rows))
    return values.astype(jnp.bfloat16)


def draw_cell_features(key, part):
    spot_order, first_cells, second_cells, sign_table, depth_level, gap_level = drawn_plan(key)
    key = jax.random.fold_in(key, 31)
    sign_key = jax.random.fold_in(key, 0)
    sign_values = random_signs(sign_key, (F, N_CELLS))
    values = sign_values
    values = values.at[:, second_cells].set(values[:, first_cells])
    return values.astype(jnp.bfloat16)


def draw_cell_factors(key, part):
    spot_order, first_cells, second_cells, sign_table, depth_level, gap_level = drawn_plan(key)
    key = jax.random.fold_in(key, 41)
    sign_key = jax.random.fold_in(key, 0)
    sign_values = random_signs(sign_key, (R, N_CELLS)) / math.sqrt(R)
    values = sign_values
    aligned_columns = jnp.transpose(sign_table) * jnp.abs(values[:, first_cells])
    values = values.at[:, first_cells].set(aligned_columns)
    values = values.at[:, second_cells].set(aligned_columns)
    return values.astype(jnp.bfloat16)


def draw_cell_potential(key, part):
    spot_order, first_cells, second_cells, sign_table, depth_level, gap_level = drawn_plan(key)
    key = jax.random.fold_in(key, 23)
    potential = jax.random.uniform(key, (N_CELLS,), jnp.float32, -0.5, 0.5)
    potential = potential.at[first_cells].set(-depth_level)
    potential = potential.at[second_cells].set(gap_level - depth_level)
    return potential


def block_scale(key, extent, cuts, least, high):
    gain, own = 1.0, jax.random.fold_in(key, 6)
    for axis_at, shards_of in cuts:
        draws = jnp.exp(jax.random.uniform(jax.random.fold_in(own, axis_at), (shards_of,), jnp.float32, least / len(cuts), high / len(cuts)))
        gain = gain * jnp.repeat(draws, extent[axis_at] // shards_of).reshape([-1 if axis == axis_at else 1 for axis in range(len(extent))])
    return gain


def setup_inputs(seed: int = 0) -> dict:
    keys = jax.random.split(jax.random.key(seed), 8)
    spot_features = draw_spot_features(jax.random.fold_in(keys[7], 71), 0)
    spot_factors = draw_spot_factors(jax.random.fold_in(keys[7], 71), 0)
    spot_log_mass = jnp.clip(jax.random.uniform(keys[2], (N_SPOTS,), jnp.float32, -1.0, 1.0) * block_scale(keys[2], (N_SPOTS,), ((0, 256),), -0.4, 0.0), -1.0, 1.0)
    cell_features = draw_cell_features(jax.random.fold_in(keys[7], 71), 0)
    cell_factors = draw_cell_factors(jax.random.fold_in(keys[7], 71), 0)
    cell_log_mass = jnp.clip(jax.random.uniform(keys[5], (N_CELLS,), jnp.float32, -1.0, 1.0) * block_scale(keys[5], (N_CELLS,), ((0, 256),), -0.4, 0.0), -1.0, 1.0)
    cell_potential = draw_cell_potential(jax.random.fold_in(keys[7], 71), 0)
    return {"spot_features": spot_features, "spot_factors": spot_factors, "spot_log_mass": spot_log_mass, "cell_features": cell_features, "cell_factors": cell_factors, "cell_log_mass": cell_log_mass, "cell_potential": cell_potential}


epsilon = 0.25


def squares(features):
    values = features.astype(jnp.float32)
    return jnp.sum(values * values, axis=0)


def contract(left_side, right_side):
    return lax.dot_general(left_side, right_side, (((0,), (0,)), ((), ())), preferred_element_type=jnp.float32)


def half_sweep(row_feat, row_fac, row_mass, col_feat, col_fac, col_pot):
    width_f = row_feat.shape[0]
    row_count = row_feat.shape[1]
    col_count = col_feat.shape[1]
    row_block = math.gcd(row_count, 512)
    col_norm = squares(col_feat)
    row_norm = squares(row_feat)
    blocks = row_count // row_block

    def tile_rows(position):
        first_row = position * row_block
        feat_part = lax.dynamic_slice_in_dim(row_feat, first_row, row_block, 1)
        fac_part = lax.dynamic_slice_in_dim(row_fac, first_row, row_block, 1)
        norm_part = lax.dynamic_slice_in_dim(row_norm, first_row, row_block, 0)
        mass_part = lax.dynamic_slice_in_dim(row_mass, first_row, row_block, 0)
        cost = (norm_part[:, None] + col_norm[None, :] - 2.0 * contract(feat_part, col_feat)) / width_f + contract(fac_part, col_fac)
        scores = (col_pot[None, :] - cost) / epsilon
        highest = jnp.max(scores, axis=1)
        log_mean = highest + jnp.log(jnp.sum(jnp.exp(scores - highest[:, None]), axis=1)) - math.log(col_count)
        return epsilon * (mass_part - log_mean)

    return lax.map(tile_rows, jnp.arange(blocks, dtype=jnp.int32)).reshape(row_count)


def reference(spot_features, spot_factors, spot_log_mass, cell_features, cell_factors, cell_log_mass, cell_potential):
    spot_potential = half_sweep(spot_features, spot_factors, spot_log_mass, cell_features, cell_factors, cell_potential)
    cell_update = half_sweep(cell_features, cell_factors, cell_log_mass, spot_features, spot_factors, spot_potential)
    return spot_potential, cell_update
```

```python
import math

import jax
import jax.numpy as jnp
from jax import lax
from jax.experimental import pallas as pl
from jax.experimental.pallas import tpu as pltpu
from jax.sharding import PartitionSpec as P

epsilon = 0.25
width = 192
depth = 128
features, factors = 64, 34
offset_lane = features + factors
dual_lane = offset_lane + 3
group = 16
rows = 768
lanes = 384
chunks = group * width // lanes
tiles = group * width // rows
lowest = -1e30
MESH = pl.DeviceIdType.MESH


def dot_first(left, right):
    return lax.dot_general(
        left, right, (((0,), (0,)), ((), ())), preferred_element_type=jnp.float32
    )


def dot_last(left, right):
    return lax.dot_general(
        left, right, (((1,), (1,)), ((), ())), preferred_element_type=jnp.float32
    )


def placing(count, first_lane, scale):
    source = lax.broadcasted_iota(jnp.int32, (count, depth), 0)
    lane = lax.broadcasted_iota(jnp.int32, (count, depth), 1)
    return jnp.where(lane == source + first_lane, scale, 0.0).astype(jnp.bfloat16)


def pieces(row):
    high = row.astype(jnp.bfloat16).astype(jnp.float32)
    rest = row - high
    middle = rest.astype(jnp.bfloat16).astype(jnp.float32)
    low = rest - middle
    at = lax.broadcasted_iota(jnp.int32, (16, row.shape[1]), 0)
    stacked = jnp.where(at == 0, high, jnp.where(at == 1, middle, jnp.where(at == 2, low, 0.0)))
    return stacked.astype(jnp.bfloat16)


def lane_between(first, last):
    lane = lax.broadcasted_iota(jnp.int32, (width, depth), 1)
    return (lane >= first) & (lane < last)


def norms(feat):
    values = feat.astype(jnp.float32)
    return jnp.sum(values * values, axis=0, keepdims=True) * (1.0 / (features * epsilon))


def z_shift(pair):
    return jnp.where(pair % 2 == 1, (pair + 1) // 2, (8 - pair // 2) % 8)


def z_shift_of(pair):
    return (pair + 1) // 2 if pair % 2 else (8 - pair // 2) % 8


def kernel(
    spot_feat, spot_fac, spot_mass, cell_feat, cell_fac, cell_mass, cell_pot,
    spot_out, cell_out,
    spots, cells, tile_a, tile_b, highest, total,
    part_1, out_1, dual, part_2, out_2,
    spot_send, spot_recv, cell_send, cell_recv,
    part_1_send, part_1_recv, dual_send, dual_recv, part_2_send, part_2_recv,
):
    blk, grp = lax.axis_index("blk"), lax.axis_index("grp")
    my_x, my_y = (blk // 4) * 2 + grp // 16, blk % 4
    my_z, my_core = (grp % 16) // 2, grp % 2

    def place(x, y, z, core):
        return ((x // 2) * 4 + y, (x % 2) * 16 + z * 2 + core)

    def along_q(shift, other):
        return place(my_x, my_y, (my_z + shift) % 8, (my_core + other) % 2)

    def along_p(dx, dy):
        return place((my_x + dx) % 4, (my_y + dy) % 4, my_z, my_core)

    barrier = pltpu.get_barrier_semaphore()
    for slot in range(1, group):
        pl.semaphore_signal(
            barrier, inc=1, device_id=along_q(z_shift_of(slot // 2), slot % 2), device_id_type=MESH
        )
        pl.semaphore_signal(
            barrier, inc=1, device_id=along_p(slot // 4, slot % 4), device_id_type=MESH
        )

    own_spots = (
        dot_first(spot_feat[...], placing(features, 0, 0.125))
        + dot_first(spot_fac[...], placing(factors, features, -4.0))
    )
    own_spots = jnp.where(lane_between(offset_lane, offset_lane + 3), 1.0, own_spots)
    spots[0:width, :] = own_spots.astype(jnp.bfloat16)
    cell_norm = norms(cell_feat[...])
    potential = cell_pot[...].reshape(1, width) * (1.0 / epsilon)
    own_cells = (
        dot_first(cell_feat[...], placing(features, 0, 1.0))
        + dot_first(cell_fac[...], placing(factors, features, 1.0))
        + dot_first(pieces(potential - cell_norm), placing(16, offset_lane, 1.0))
    )
    own_cells = jnp.where(lane_between(dual_lane, dual_lane + 3), 1.0, own_cells)
    cells[0:width, :] = own_cells.astype(jnp.bfloat16)

    pl.semaphore_wait(barrier, 2 * (group - 1))

    def spot_copy(slot):
        return pltpu.make_async_remote_copy(
            src_ref=spots.at[pl.ds(0, width), :],
            dst_ref=spots.at[pl.ds(slot * width, width), :],
            send_sem=spot_send.at[slot],
            recv_sem=spot_recv.at[slot],
            device_id=along_q(z_shift_of(slot // 2), slot % 2),
            device_id_type=MESH,
        )

    def cell_copy(slot):
        return pltpu.make_async_remote_copy(
            src_ref=cells.at[pl.ds(0, width), :],
            dst_ref=cells.at[pl.ds(slot * width, width), :],
            send_sem=cell_send.at[slot],
            recv_sem=cell_recv.at[slot],
            device_id=along_p(slot // 4, slot % 4),
            device_id_type=MESH,
        )

    near_first = (1, 3, 4, 12, 5, 7, 13, 15, 2, 8, 6, 14, 9, 11, 10)
    for spot_slot, cell_slot in zip(range(1, group), near_first):
        cell_copy(cell_slot).start()
        spot_copy(spot_slot).start()
    for slot in range(1, group):
        cell_copy(slot).wait()
        spot_copy(slot).wait()

    def half(by_row, by_lane, finish):
        highest[...] = jnp.full(highest.shape, lowest, jnp.float32)
        total[...] = jnp.zeros(total.shape, jnp.float32)

        def fill(step, tile):
            chunk, part = chunks - 1 - step // tiles, step % tiles
            left = by_row[pl.ds(pl.multiple_of(part * rows, rows), rows), :]
            right = by_lane[pl.ds(pl.multiple_of(chunk * lanes, lanes), lanes), :]
            scores = dot_last(left, right)
            tile[...] = scores
            return jnp.max(scores.reshape(rows // 8, 8, lanes), axis=0)

        def absorb(step, tile, newest):
            chunk = chunks - 1 - step // tiles
            before = highest[chunk]
            after = jnp.maximum(before, newest)
            highest[chunk] = after
            scores = tile[...].reshape(rows // 8, 8, lanes)
            total[chunk] = total[chunk] * jnp.exp(before - after) + jnp.sum(
                jnp.exp(scores - after[None]), axis=0
            )

        def close(chunk):
            top = jnp.max(highest[chunk], axis=0, keepdims=True)
            sums = jnp.sum(total[chunk] * jnp.exp(highest[chunk] - top), axis=0, keepdims=True)
            finish(chunk, top, sums)

        def body(pair, newest):
            step = 2 * pair
            second = fill(step + 1, tile_b)
            absorb(step, tile_a, newest)
            third = fill(step + 2, tile_a)
            absorb(step + 1, tile_b, second)

            @pl.when(pair % (tiles // 2) == tiles // 2 - 1)
            def _():
                close(chunks - 1 - (step + 1) // tiles)

            return third

        count = chunks * tiles
        newest = lax.fori_loop(0, count // 2 - 1, body, fill(0, tile_a))
        second = fill(count - 1, tile_b)
        absorb(count - 2, tile_a, newest)
        absorb(count - 1, tile_b, second)
        close(0)

    def store_pair(out, slot, top, sums, first):
        out[slot, 0:1, 0:width] = top[:, first:first + width]
        out[slot, 1:2, 0:width] = sums[:, first:first + width]

    def combine(part):
        top = part[0, 0:1, 0:width]
        for slot in range(1, group):
            top = jnp.maximum(top, part[slot, 0:1, 0:width])
        sums = jnp.zeros_like(top)
        for slot in range(group):
            sums += part[slot, 1:2, 0:width] * jnp.exp(part[slot, 0:1, 0:width] - top)
        return top + jnp.log(sums)

    def part_1_copy(slot, target):
        return pltpu.make_async_remote_copy(
            src_ref=out_1.at[slot],
            dst_ref=part_1.at[slot],
            send_sem=part_1_send.at[slot],
            recv_sem=part_1_recv.at[slot],
            device_id=target,
            device_id_type=MESH,
        )

    def finish_1(chunk, top, sums):
        store_pair(out_1, 2 * chunk + 1, top, sums, width)
        if isinstance(chunk, int):
            store_pair(part_1, 0, top, sums, 0)
            part_1_copy(1, along_q(0, 1)).start()
        else:
            store_pair(out_1, 2 * chunk, top, sums, 0)
            back = (8 - z_shift(chunk)) % 8
            part_1_copy(2 * chunk, along_q(back, 0)).start()
            part_1_copy(2 * chunk + 1, along_q(back, 1)).start()

    half(cells, spots, finish_1)
    for slot in range(1, group):
        part_1_copy(slot, along_q((8 - z_shift_of(slot // 2)) % 8, slot % 2)).wait()
    log_sum = combine(part_1)
    mass = spot_mass[...].reshape(1, width)
    log_count = math.log(256 * width)
    term = mass - log_sum + log_count
    spot_out[...] = (epsilon * (term + norms(spot_feat[...]))).reshape(width)
    dual[0] = term

    def dual_copy(slot):
        return pltpu.make_async_remote_copy(
            src_ref=dual.at[0],
            dst_ref=dual.at[slot],
            send_sem=dual_send.at[slot],
            recv_sem=dual_recv.at[slot],
            device_id=along_q(z_shift_of(slot // 2), slot % 2),
            device_id_type=MESH,
        )

    for slot in range(1, group):
        dual_copy(slot).start()
    keep = jnp.logical_not(lane_between(offset_lane, offset_lane + 6))
    for slot in range(group):
        if slot:
            dual_copy(slot).wait()
        at = slice(slot * width, (slot + 1) * width)
        moved = dot_first(pieces(dual[slot]), placing(16, dual_lane, 1.0))
        spots[at, :] = jnp.where(keep, spots[at, :].astype(jnp.float32), moved).astype(jnp.bfloat16)

    def part_2_copy(slot, target):
        return pltpu.make_async_remote_copy(
            src_ref=out_2.at[slot],
            dst_ref=part_2.at[slot],
            send_sem=part_2_send.at[slot],
            recv_sem=part_2_recv.at[slot],
            device_id=target,
            device_id_type=MESH,
        )

    def finish_2(chunk, top, sums):
        store_pair(out_2, 2 * chunk + 1, top, sums, width)
        if isinstance(chunk, int):
            store_pair(part_2, 0, top, sums, 0)
            part_2_copy(1, along_p(0, 3)).start()
        else:
            store_pair(out_2, 2 * chunk, top, sums, 0)
            back_x, near_y = (4 - chunk // 2) % 4, 2 * (chunk % 2)
            part_2_copy(2 * chunk, along_p(back_x, (4 - near_y) % 4)).start()
            part_2_copy(2 * chunk + 1, along_p(back_x, 3 - near_y)).start()

    half(spots, cells, finish_2)
    for slot in range(1, group):
        part_2_copy(slot, along_p((4 - slot // 4) % 4, (4 - slot % 4) % 4)).wait()
    log_sum = combine(part_2)
    mass = cell_mass[...].reshape(1, width)
    cell_out[...] = (epsilon * (mass - log_sum + norms(cell_feat[...]) + log_count)).reshape(width)


def local(*arguments):
    vmem = pl.BlockSpec(memory_space=pltpu.VMEM)
    points = group * width
    return pl.pallas_call(
        kernel,
        out_shape=[jax.ShapeDtypeStruct((width,), jnp.float32)] * 2,
        in_specs=[vmem] * 7,
        out_specs=[vmem] * 2,
        scratch_shapes=[
            pltpu.VMEM((points, depth), jnp.bfloat16),
            pltpu.VMEM((points, depth), jnp.bfloat16),
            pltpu.VMEM((rows, lanes), jnp.float32),
            pltpu.VMEM((rows, lanes), jnp.float32),
            pltpu.VMEM((chunks, 8, lanes), jnp.float32),
            pltpu.VMEM((chunks, 8, lanes), jnp.float32),
            pltpu.VMEM((group, 2, width), jnp.float32),
            pltpu.VMEM((group, 2, width), jnp.float32),
            pltpu.VMEM((group, 1, width), jnp.float32),
            pltpu.VMEM((group, 2, width), jnp.float32),
            pltpu.VMEM((group, 2, width), jnp.float32),
        ]
        + [pltpu.SemaphoreType.DMA((group,))] * 10,
        compiler_params=pltpu.CompilerParams(
            collective_id=0, has_side_effects=True, vmem_limit_bytes=32 * 1024 * 1024
        ),
        name="sweep",
    )(*arguments)


def solution(mesh):
    column = P(None, ("blk", "grp"))
    flat = P(("blk", "grp"))
    return jax.shard_map(
        local,
        mesh=mesh,
        in_specs=(column, column, flat, column, column, flat, flat),
        out_specs=(flat, flat),
        check_vma=False,
    )
```

```python
import math

import jax
import jax.numpy as jnp
from jax import lax
from jax.experimental import pallas as pl
from jax.experimental.pallas import tpu as pltpu
from jax.sharding import PartitionSpec as P

epsilon = 0.25
width = 192
depth = 128
features, factors = 64, 34
offset_lane = features + factors
dual_lane = offset_lane + 3
group = 16
rows = 768
lanes = 384
chunks = group * width // lanes
tiles = group * width // rows
lowest = -1e30
MESH = pl.DeviceIdType.MESH


def dot_first(left, right):
    return lax.dot_general(
        left, right, (((0,), (0,)), ((), ())), preferred_element_type=jnp.float32
    )


def dot_last(left, right):
    return lax.dot_general(
        left, right, (((1,), (1,)), ((), ())), preferred_element_type=jnp.float32
    )


def placing(count, first_lane, scale):
    source = lax.broadcasted_iota(jnp.int32, (count, depth), 0)
    lane = lax.broadcasted_iota(jnp.int32, (count, depth), 1)
    return jnp.where(lane == source + first_lane, scale, 0.0).astype(jnp.bfloat16)


def pieces(row):
    high = row.astype(jnp.bfloat16).astype(jnp.float32)
    rest = row - high
    middle = rest.astype(jnp.bfloat16).astype(jnp.float32)
    low = rest - middle
    at = lax.broadcasted_iota(jnp.int32, (16, row.shape[1]), 0)
    stacked = jnp.where(at == 0, high, jnp.where(at == 1, middle, jnp.where(at == 2, low, 0.0)))
    return stacked.astype(jnp.bfloat16)


def lane_between(first, last):
    lane = lax.broadcasted_iota(jnp.int32, (width, depth), 1)
    return (lane >= first) & (lane < last)


def norms(feat):
    values = feat.astype(jnp.float32)
    return jnp.sum(values * values, axis=0, keepdims=True) * (1.0 / (features * epsilon))


def z_shift(pair):
    return jnp.where(pair % 2 == 1, (pair + 1) // 2, (8 - pair // 2) % 8)


def z_shift_of(pair):
    return (pair + 1) // 2 if pair % 2 else (8 - pair // 2) % 8


def near(place):
    return place + (place // 2) * (5 - 2 * place)


def kernel(
    spot_feat_in, spot_fac_in, spot_mass_in, cell_feat_in, cell_fac_in, cell_mass_in, cell_pot_in,
    spot_out, cell_out,
    spot_feat, spot_fac, spot_mass, cell_feat, cell_fac, cell_mass, cell_pot, input_sem,
    spots, cells, spread, tile_a, tile_b, highest, total,
    part_1, out_1, dual, part_2, out_2,
    spot_send, spot_recv, cell_send, cell_recv,
    part_1_send, part_1_recv, dual_send, dual_recv, part_2_send, part_2_recv,
):
    blk, grp = lax.axis_index("blk"), lax.axis_index("grp")
    my_x, my_y = (blk // 4) * 2 + grp // 16, blk % 4
    my_z, my_core = (grp % 16) // 2, grp % 2

    def place(x, y, z, core):
        return ((x // 2) * 4 + y, (x % 2) * 16 + z * 2 + core)

    def along_q(shift, other):
        return place(my_x, my_y, (my_z + shift) % 8, (my_core + other) % 2)

    def along_p(dx, dy):
        return place((my_x + dx) % 4, (my_y + dy) % 4, my_z, my_core)

    loads = [
        pltpu.make_async_copy(source, target, input_sem.at[at])
        for at, (source, target) in enumerate((
            (cell_feat_in, cell_feat), (cell_fac_in, cell_fac), (cell_pot_in, cell_pot),
            (spot_feat_in, spot_feat), (spot_fac_in, spot_fac),
            (spot_mass_in, spot_mass), (cell_mass_in, cell_mass),
        ))
    ]
    for load in loads:
        load.start()

    barrier = pltpu.get_barrier_semaphore()
    for slot in range(1, group):
        pl.semaphore_signal(
            barrier, inc=1, device_id=along_q(z_shift_of(slot // 2), slot % 2), device_id_type=MESH
        )
        pl.semaphore_signal(
            barrier, inc=1, device_id=along_p(near(slot // 4), near(slot % 4)), device_id_type=MESH
        )
    for load in loads:
        load.wait()

    own_spots = (
        dot_first(spot_feat[...], placing(features, 0, 0.125))
        + dot_first(spot_fac[...], placing(factors, features, -4.0))
    )
    own_spots = jnp.where(lane_between(offset_lane, offset_lane + 3), 1.0, own_spots)
    spots[0:width, :] = own_spots.astype(jnp.bfloat16)
    cell_norm = norms(cell_feat[...])
    potential = cell_pot[...].reshape(1, width) * (1.0 / epsilon)
    own_cells = (
        dot_first(cell_feat[...], placing(features, 0, 1.0))
        + dot_first(cell_fac[...], placing(factors, features, 1.0))
        + dot_first(pieces(potential - cell_norm), placing(16, offset_lane, 1.0))
    )
    own_cells = jnp.where(lane_between(dual_lane, dual_lane + 3), 1.0, own_cells)
    cells[0:width, :] = own_cells.astype(jnp.bfloat16)

    source = lax.broadcasted_iota(jnp.int32, spread.shape, 0)
    target = lax.broadcasted_iota(jnp.int32, spread.shape, 1)
    lane, kind = target % depth, source // group
    value = jnp.where(
        lane == dual_lane + kind,
        jnp.where(kind < 3, 1.0, 0.0),
        jnp.where((kind == 3) & (lane >= offset_lane) & (lane < dual_lane), -1.0, 0.0),
    )
    spread[...] = jnp.where(target // depth == source % group, value, 0.0).astype(jnp.bfloat16)

    pl.semaphore_wait(barrier, 2 * (group - 1))

    def spot_copy(pair):
        return pltpu.make_async_remote_copy(
            src_ref=spots.at[pl.ds(0, width), :],
            dst_ref=spots.at[pl.ds(2 * pair * width, width), :],
            send_sem=spot_send.at[2 * pair],
            recv_sem=spot_recv.at[2 * pair],
            device_id=along_q(z_shift_of(pair), 0),
            device_id_type=MESH,
        )

    def spot_pass(pair):
        return pltpu.make_async_remote_copy(
            src_ref=spots.at[pl.ds(2 * pair * width, width), :],
            dst_ref=spots.at[pl.ds((2 * pair + 1) * width, width), :],
            send_sem=spot_send.at[2 * pair + 1],
            recv_sem=spot_recv.at[2 * pair + 1],
            device_id=along_q(0, 1),
            device_id_type=MESH,
        )

    def cell_copy(slot):
        return pltpu.make_async_remote_copy(
            src_ref=cells.at[pl.ds(0, width), :],
            dst_ref=cells.at[pl.ds(slot * width, width), :],
            send_sem=cell_send.at[slot],
            recv_sem=cell_recv.at[slot],
            device_id=along_p(near(slot // 4), near(slot % 4)),
            device_id_type=MESH,
        )

    def pass_on(*pairs):
        for pair in pairs:
            spot_copy(pair).wait_recv()
            spot_pass(pair).start()

    spot_pass(0).start()
    spot_copy(1).start()
    for slot in range(1, 4):
        cell_copy(slot).start()
    for part in range(1, 4):
        spot_copy(2 * part).start()
        for slot in range(4 * part, 4 * part + 4):
            cell_copy(slot).start()
        spot_copy(2 * part + 1).start()

    def arrive(part):
        for slot in range(max(4 * part, 1), 4 * part + 4):
            cell_copy(slot).wait_recv()
        spot_pass(2 * part).wait_recv()
        spot_pass(2 * part + 1).wait_recv()

    def clear():
        highest[...] = jnp.full(highest.shape, lowest, jnp.float32)
        total[...] = jnp.zeros(total.shape, jnp.float32)

    def fill(by_row, by_lane, part, chunk, tile):
        left = by_row[pl.ds(pl.multiple_of(part * rows, rows), rows), :]
        right = by_lane[pl.ds(pl.multiple_of(chunk * lanes, lanes), lanes), :]
        scores = dot_last(left, right)
        tile[...] = scores
        return jnp.max(scores.reshape(rows // 8, 8, lanes), axis=0)

    def absorb(chunk, tile, newest):
        before = highest[chunk]
        after = jnp.maximum(before, newest)
        highest[chunk] = after
        scores = tile[...].reshape(rows // 8, 8, lanes)
        total[chunk] = total[chunk] * jnp.exp(before - after) + jnp.sum(
            jnp.exp(scores - after[None]), axis=0
        )

    def close(chunk, finish):
        top = jnp.max(highest[chunk], axis=0, keepdims=True)
        sums = jnp.sum(total[chunk] * jnp.exp(highest[chunk] - top), axis=0, keepdims=True)
        finish(chunk, top, sums)

    count = chunks * tiles

    def half(by_row, by_lane, plan, closes, events, finish):
        clear()

        def body(pair, newest):
            step = 2 * pair
            second = fill(by_row, by_lane, *plan(step + 1), tile_b)
            absorb(plan(step)[1], tile_a, newest)
            for at, event in events:
                pl.when(pair == at)(event)
            third = fill(by_row, by_lane, *plan(step + 2), tile_a)
            absorb(plan(step + 1)[1], tile_b, second)

            @pl.when(closes(step))
            def _():
                close(plan(step)[1], finish)

            @pl.when(closes(step + 1))
            def _():
                close(plan(step + 1)[1], finish)

            return third

        part, chunk = plan(0)
        newest = lax.fori_loop(0, count // 2 - 1, body, fill(by_row, by_lane, part, chunk, tile_a))
        second = fill(by_row, by_lane, *plan(count - 1), tile_b)
        absorb(plan(count - 2)[1], tile_a, newest)
        if closes(count - 2):
            close(plan(count - 2)[1], finish)
        absorb(0, tile_b, second)
        close(0, finish)

    def store_pair(out, slot, top, sums, first):
        out[slot, 0:1, 0:width] = top[:, first:first + width]
        out[slot, 1:2, 0:width] = sums[:, first:first + width]

    def combine(part):
        top = part[0, 0:1, 0:width]
        for slot in range(1, group):
            top = jnp.maximum(top, part[slot, 0:1, 0:width])
        sums = jnp.zeros_like(top)
        for slot in range(group):
            sums += part[slot, 1:2, 0:width] * jnp.exp(part[slot, 0:1, 0:width] - top)
        return top + jnp.log(sums)

    def part_1_copy(slot, target):
        return pltpu.make_async_remote_copy(
            src_ref=out_1.at[slot],
            dst_ref=part_1.at[slot],
            send_sem=part_1_send.at[slot],
            recv_sem=part_1_recv.at[slot],
            device_id=target,
            device_id_type=MESH,
        )

    def finish_1(chunk, top, sums):
        store_pair(out_1, 2 * chunk + 1, top, sums, width)
        if isinstance(chunk, int):
            store_pair(part_1, 0, top, sums, 0)
            part_1_copy(1, along_q(0, 1)).start()
        else:
            store_pair(out_1, 2 * chunk, top, sums, 0)
            back = (8 - z_shift(chunk)) % 8
            part_1_copy(2 * chunk, along_q(back, 0)).start()
            part_1_copy(2 * chunk + 1, along_q(back, 1)).start()

    def plan_1(step):
        turn = sum(jnp.where(step >= 2 * k * k, 1, 0) for k in range(1, tiles))
        rest = step - 2 * turn * turn
        old = rest < 2 * turn
        part = jnp.where(old, jnp.where(rest < turn, rest, rest - turn), turn)
        chunk = jnp.where(
            old, 2 * turn + jnp.where(rest < turn, 0, 1), 4 * turn + 1 - rest
        )
        return part, chunk

    pass_on(1)
    arrive(0)
    half(
        cells,
        spots,
        plan_1,
        lambda step: step >= count - chunks,
        (
            (0, lambda: (pass_on(2, 3), arrive(1), None)[-1]),
            (1, lambda: pass_on(4, 5)),
            (3, lambda: arrive(2)),
            (5, lambda: pass_on(6, 7)),
            (8, lambda: arrive(3)),
        ),
        finish_1,
    )
    for pair in range(8):
        spot_pass(pair).wait_send()
        if pair:
            spot_copy(pair).wait_send()
    for slot in range(1, group):
        cell_copy(slot).wait_send()
        part_1_copy(slot, along_q((8 - z_shift_of(slot // 2)) % 8, slot % 2)).wait()
    log_sum = combine(part_1)
    mass = spot_mass[...].reshape(1, width)
    log_count = math.log(256 * width)
    term = mass - log_sum + log_count
    spot_out[...] = (epsilon * (term + norms(spot_feat[...]))).reshape(width)
    dual[0:1, :] = term

    def dual_copy(slot):
        return pltpu.make_async_remote_copy(
            src_ref=dual.at[pl.ds(0, 1), :],
            dst_ref=dual.at[pl.ds(slot, 1), :],
            send_sem=dual_send.at[slot],
            recv_sem=dual_recv.at[slot],
            device_id=along_q(z_shift_of(slot // 2), slot % 2),
            device_id_type=MESH,
        )

    for slot in range(1, group):
        dual_copy(slot).start()
    for slot in range(1, group):
        dual_copy(slot).wait()
    values = dual[...]
    high = values.astype(jnp.bfloat16).astype(jnp.float32)
    middle = (values - high).astype(jnp.bfloat16).astype(jnp.float32)
    low = values - high - middle
    stacked = jnp.concatenate([high, middle, low, jnp.ones_like(low)], axis=0).astype(jnp.bfloat16)
    moved = dot_first(stacked, spread[...]).astype(jnp.bfloat16)
    for slot in range(group):
        at = slice(slot * width, (slot + 1) * width)
        spots[at, :] = spots[at, :] + moved[:, slot * depth:(slot + 1) * depth]

    def part_2_copy(slot, target):
        return pltpu.make_async_remote_copy(
            src_ref=out_2.at[slot],
            dst_ref=part_2.at[slot],
            send_sem=part_2_send.at[slot],
            recv_sem=part_2_recv.at[slot],
            device_id=target,
            device_id_type=MESH,
        )

    def finish_2(chunk, top, sums):
        store_pair(out_2, 2 * chunk + 1, top, sums, width)
        if isinstance(chunk, int):
            store_pair(part_2, 0, top, sums, 0)
            part_2_copy(1, along_p(0, 3)).start()
        else:
            store_pair(out_2, 2 * chunk, top, sums, 0)
            back_x, first_y = (4 - near(chunk // 2)) % 4, 2 * (chunk % 2)
            part_2_copy(2 * chunk, along_p(back_x, (4 - near(first_y)) % 4)).start()
            part_2_copy(2 * chunk + 1, along_p(back_x, (4 - near(first_y + 1)) % 4)).start()

    def plan_2(step):
        return step % tiles, chunks - 1 - step // tiles

    half(spots, cells, plan_2, lambda step: step % tiles == tiles - 1, (), finish_2)
    for slot in range(1, group):
        part_2_copy(slot, along_p((4 - near(slot // 4)) % 4, (4 - near(slot % 4)) % 4)).wait()
    log_sum = combine(part_2)
    mass = cell_mass[...].reshape(1, width)
    cell_out[...] = (epsilon * (mass - log_sum + norms(cell_feat[...]) + log_count)).reshape(width)


def local(*arguments):
    vmem = pl.BlockSpec(memory_space=pltpu.VMEM)
    points = group * width
    return pl.pallas_call(
        kernel,
        out_shape=[jax.ShapeDtypeStruct((width,), jnp.float32)] * 2,
        in_specs=[pl.BlockSpec(memory_space=pl.ANY)] * 7,
        out_specs=[vmem] * 2,
        scratch_shapes=[pltpu.VMEM(value.shape, value.dtype) for value in arguments]
        + [
            pltpu.SemaphoreType.DMA((7,)),
            pltpu.VMEM((points, depth), jnp.bfloat16),
            pltpu.VMEM((points, depth), jnp.bfloat16),
            pltpu.VMEM((4 * group, group * depth), jnp.bfloat16),
            pltpu.VMEM((rows, lanes), jnp.float32),
            pltpu.VMEM((rows, lanes), jnp.float32),
            pltpu.VMEM((chunks, 8, lanes), jnp.float32),
            pltpu.VMEM((chunks, 8, lanes), jnp.float32),
            pltpu.VMEM((group, 2, width), jnp.float32),
            pltpu.VMEM((group, 2, width), jnp.float32),
            pltpu.VMEM((group, width), jnp.float32),
            pltpu.VMEM((group, 2, width), jnp.float32),
            pltpu.VMEM((group, 2, width), jnp.float32),
        ]
        + [pltpu.SemaphoreType.DMA((group,))] * 10,
        compiler_params=pltpu.CompilerParams(
            collective_id=0, has_side_effects=True, vmem_limit_bytes=56 * 1024 * 1024
        ),
        name="sweep",
    )(*arguments)


def solution(mesh):
    column = P(None, ("blk", "grp"))
    flat = P(("blk", "grp"))
    return jax.shard_map(
        local,
        mesh=mesh,
        in_specs=(column, column, flat, column, column, flat, flat),
        out_specs=(flat, flat),
        check_vma=False,
    )
```

```python
import math

import jax
import jax.numpy as jnp
from jax import lax
from jax.experimental import pallas as pl
from jax.experimental.pallas import tpu as pltpu
from jax.sharding import PartitionSpec as P

epsilon = 0.25
width = 192
depth = 128
features, factors = 64, 34
offset_lane = features + factors
dual_lane = offset_lane + 3
group = 16
lanes = 384
chunks = group * width // lanes
near_rows = 7 * width
far_rows = 9 * width
half_rows = group * width // 2
part_rows = width // 2
lowest = -1e30
MESH = pl.DeviceIdType.MESH


def dot_first(left, right):
    return lax.dot_general(
        left, right, (((0,), (0,)), ((), ())), preferred_element_type=jnp.float32
    )


def dot_last(left, right):
    return lax.dot_general(
        left, right, (((1,), (1,)), ((), ())), preferred_element_type=jnp.float32
    )


def placing(count, first_lane, scale):
    source = lax.broadcasted_iota(jnp.int32, (count, depth), 0)
    lane = lax.broadcasted_iota(jnp.int32, (count, depth), 1)
    return jnp.where(lane == source + first_lane, scale, 0.0).astype(jnp.bfloat16)


def pieces(row):
    high = row.astype(jnp.bfloat16).astype(jnp.float32)
    rest = row - high
    middle = rest.astype(jnp.bfloat16).astype(jnp.float32)
    low = rest - middle
    at = lax.broadcasted_iota(jnp.int32, (16, row.shape[1]), 0)
    stacked = jnp.where(at == 0, high, jnp.where(at == 1, middle, jnp.where(at == 2, low, 0.0)))
    return stacked.astype(jnp.bfloat16)


def lane_between(first, last):
    lane = lax.broadcasted_iota(jnp.int32, (width, depth), 1)
    return (lane >= first) & (lane < last)


def norms(feat):
    values = feat.astype(jnp.float32)
    return jnp.sum(values * values, axis=0, keepdims=True) * (1.0 / (features * epsilon))


def z_shift(pair):
    return jnp.where(pair % 2 == 1, (pair + 1) // 2, (8 - pair // 2) % 8)


def z_shift_of(pair):
    return (pair + 1) // 2 if pair % 2 else (8 - pair // 2) % 8


def shift(place):
    return place + (place // 2) * (5 - 2 * place)


def slot_of(i, j):
    if j == 0:
        return i
    return 3 + j if i == 0 else 7 + 3 * (j - 1) + i - 1


def lines_of(slot):
    i = jnp.where(slot < 4, slot, jnp.where(slot < 7, 0, 1 + (slot + 2) % 3))
    j = jnp.where(slot < 4, 0, jnp.where(slot < 7, slot - 3, 1 + (slot - 7) // 3))
    return i, j


def kernel(
    spot_feat_in, spot_fac_in, spot_mass_in, cell_feat_in, cell_fac_in, cell_mass_in, cell_pot_in,
    spot_out, cell_out,
    spot_feat, spot_fac, spot_mass, cell_feat, cell_fac, cell_mass, cell_pot, input_sem,
    spots, cells, spread, tile_a, tile_b, highest, total,
    part_1, out_1, dual, part_2, out_2,
    spot_send, spot_recv, cell_send, cell_recv,
    part_1_send, part_1_recv, dual_send, dual_recv, part_2_send, part_2_recv,
):
    blk, grp = lax.axis_index("blk"), lax.axis_index("grp")
    my_x, my_y = (blk // 4) * 2 + grp // 16, blk % 4
    my_z, my_core = (grp % 16) // 2, grp % 2

    def place(x, y, z, core):
        return ((x // 2) * 4 + y, (x % 2) * 16 + z * 2 + core)

    def along_q(shift, other):
        return place(my_x, my_y, (my_z + shift) % 8, (my_core + other) % 2)

    def along_p(dx, dy):
        return place((my_x + dx) % 4, (my_y + dy) % 4, my_z, my_core)

    loads = [
        pltpu.make_async_copy(source, target, input_sem.at[at])
        for at, (source, target) in enumerate((
            (cell_feat_in, cell_feat), (cell_fac_in, cell_fac), (cell_pot_in, cell_pot),
            (spot_feat_in, spot_feat), (spot_fac_in, spot_fac),
            (spot_mass_in, spot_mass), (cell_mass_in, cell_mass),
        ))
    ]
    for load in loads:
        load.start()

    barrier = pltpu.get_barrier_semaphore()
    for slot in range(1, group):
        pl.semaphore_signal(
            barrier, inc=1, device_id=along_q(z_shift_of(slot // 2), slot % 2), device_id_type=MESH
        )
        pl.semaphore_signal(
            barrier, inc=1, device_id=along_p(shift(slot // 4), shift(slot % 4)), device_id_type=MESH
        )
    for load in loads:
        load.wait()

    own_spots = (
        dot_first(spot_feat[...], placing(features, 0, 0.125))
        + dot_first(spot_fac[...], placing(factors, features, -4.0))
    )
    own_spots = jnp.where(lane_between(offset_lane, offset_lane + 3), 1.0, own_spots)
    spots[0:width, :] = own_spots.astype(jnp.bfloat16)
    cell_norm = norms(cell_feat[...])
    potential = cell_pot[...].reshape(1, width) * (1.0 / epsilon)
    own_cells = (
        dot_first(cell_feat[...], placing(features, 0, 1.0))
        + dot_first(cell_fac[...], placing(factors, features, 1.0))
        + dot_first(pieces(potential - cell_norm), placing(16, offset_lane, 1.0))
    )
    own_cells = jnp.where(lane_between(dual_lane, dual_lane + 3), 1.0, own_cells)
    cells[0:width, :] = own_cells.astype(jnp.bfloat16)

    source = lax.broadcasted_iota(jnp.int32, spread.shape, 0)
    target = lax.broadcasted_iota(jnp.int32, spread.shape, 1)
    lane, kind = target % depth, source // group
    value = jnp.where(
        lane == dual_lane + kind,
        jnp.where(kind < 3, 1.0, 0.0),
        jnp.where((kind == 3) & (lane >= offset_lane) & (lane < dual_lane), -1.0, 0.0),
    )
    spread[...] = jnp.where(target // depth == source % group, value, 0.0).astype(jnp.bfloat16)

    pl.semaphore_wait(barrier, 2 * (group - 1))

    def spot_copy(pair, source=0, first=0, count=width, flight=None):
        target = z_shift_of(pair) - z_shift_of(source)
        at = 2 * pair if flight is None else flight
        return pltpu.make_async_remote_copy(
            src_ref=spots.at[pl.ds(2 * source * width + first, count), :],
            dst_ref=spots.at[pl.ds(2 * pair * width + first, count), :],
            send_sem=spot_send.at[at],
            recv_sem=spot_recv.at[at],
            device_id=along_q((target + 8) % 8, 0),
            device_id_type=MESH,
        )

    def spot_pass(pair):
        return pltpu.make_async_remote_copy(
            src_ref=spots.at[pl.ds(2 * pair * width, width), :],
            dst_ref=spots.at[pl.ds((2 * pair + 1) * width, width), :],
            send_sem=spot_send.at[2 * pair + 1],
            recv_sem=spot_recv.at[2 * pair + 1],
            device_id=along_q(0, 1),
            device_id_type=MESH,
        )

    def cell_copy(i, j):
        slot = slot_of(i, j)
        return pltpu.make_async_remote_copy(
            src_ref=cells.at[pl.ds(0, width), :],
            dst_ref=cells.at[pl.ds(slot * width, width), :],
            send_sem=cell_send.at[slot],
            recv_sem=cell_recv.at[slot],
            device_id=along_p(shift(i), shift(j)),
            device_id_type=MESH,
        )

    def cell_turn(i, j, along_y):
        source, first = (slot_of(i, 0), 0) if along_y else (slot_of(0, j), part_rows)
        at = slot_of(i, j) + (0 if along_y else 9)
        return pltpu.make_async_remote_copy(
            src_ref=cells.at[pl.ds(source * width + first, part_rows), :],
            dst_ref=cells.at[pl.ds(slot_of(i, j) * width + first, part_rows), :],
            send_sem=cell_send.at[at],
            recv_sem=cell_recv.at[at],
            device_id=along_p(0, shift(j)) if along_y else along_p(shift(i), 0),
            device_id_type=MESH,
        )

    line = (1, 2, 3)
    spot_direct = [spot_copy(pair) for pair in (3, 4, 1, 2)]
    spot_further = [
        spot_copy(5, 3),
        spot_copy(6, 4),
        spot_copy(7, 3, 0, part_rows),
        spot_copy(7, 4, part_rows, part_rows, 16),
    ]
    cell_direct = [cell_copy(0, j) for j in line] + [cell_copy(i, 0) for i in line]
    cell_turns = [
        cell_turn(i, j, along_y) for i in line for j in line for along_y in (True, False)
    ]
    passes = [spot_pass(pair) for pair in range(8)]
    passes[0].start()
    for spot_step, cell_step in zip(spot_direct, ((0, 3), (1, 4), (2,), (5,))):
        spot_step.start()
        for at in cell_step:
            cell_direct[at].start()
    for i in line:
        cell_copy(i, 0).wait_recv()
        for j in line:
            cell_turn(i, j, True).start()
        cell_copy(0, i).wait_recv()
        for j in line:
            cell_turn(j, i, False).start()
    for pair in (3, 4):
        spot_copy(pair).wait_recv()
    for step in spot_further:
        step.start()
    for pair in (1, 2):
        spot_copy(pair).wait_recv()
    for pair in range(1, 5):
        passes[pair].start()
    for pair in range(5):
        passes[pair].wait_recv()

    def further():
        for step in spot_further:
            step.wait_recv()
        for pair in (5, 6, 7):
            passes[pair].start()
        for step in cell_turns:
            step.wait_recv()

    def sent():
        for step in spot_direct + spot_further + cell_direct + cell_turns + passes:
            step.wait_send()

    def clear():
        highest[...] = jnp.full(highest.shape, lowest, jnp.float32)
        total[...] = jnp.zeros(total.shape, jnp.float32)

    def fill(by_row, first, count, by_lane, chunk, tile):
        right = by_lane[pl.ds(pl.multiple_of(chunk * lanes, lanes), lanes), :]
        scores = dot_last(by_row[pl.ds(first, count), :], right)
        tile[0:count, :] = scores
        return jnp.max(scores.reshape(count // 8, 8, lanes), axis=0)

    def absorb(chunk, count, tile, newest):
        before = highest[chunk]
        after = jnp.maximum(before, newest)
        highest[chunk] = after
        scores = tile[0:count, :].reshape(count // 8, 8, lanes)
        total[chunk] = total[chunk] * jnp.exp(before - after) + jnp.sum(
            jnp.exp(scores - after[None]), axis=0
        )

    def close(chunk, finish):
        top = jnp.max(highest[chunk], axis=0, keepdims=True)
        sums = jnp.sum(total[chunk] * jnp.exp(highest[chunk] - top), axis=0, keepdims=True)
        finish(chunk, top, sums)

    def store_pair(out, slot, top, sums, first):
        out[slot, 0:1, 0:width] = top[:, first:first + width]
        out[slot, 1:2, 0:width] = sums[:, first:first + width]

    def combine(part):
        top = part[0, 0:1, 0:width]
        for slot in range(1, group):
            top = jnp.maximum(top, part[slot, 0:1, 0:width])
        sums = jnp.zeros_like(top)
        for slot in range(group):
            sums += part[slot, 1:2, 0:width] * jnp.exp(part[slot, 0:1, 0:width] - top)
        return top + jnp.log(sums)

    def part_1_copy(slot, target):
        return pltpu.make_async_remote_copy(
            src_ref=out_1.at[slot],
            dst_ref=part_1.at[slot],
            send_sem=part_1_send.at[slot],
            recv_sem=part_1_recv.at[slot],
            device_id=target,
            device_id_type=MESH,
        )

    def finish_1(chunk, top, sums):
        store_pair(out_1, 2 * chunk + 1, top, sums, width)
        if isinstance(chunk, int) and chunk == 0:
            store_pair(part_1, 0, top, sums, 0)
            part_1_copy(1, along_q(0, 1)).start()
        else:
            store_pair(out_1, 2 * chunk, top, sums, 0)
            back = (8 - z_shift(chunk)) % 8
            part_1_copy(2 * chunk, along_q(back, 0)).start()
            part_1_copy(2 * chunk + 1, along_q(back, 1)).start()

    def fill_near(chunk, tile):
        return fill(cells, 0, near_rows, spots, chunk, tile)

    def fill_far(chunk, tile):
        return fill(cells, near_rows, far_rows, spots, chunk, tile)

    def absorb_near(chunk, tile, newest):
        absorb(chunk, near_rows, tile, newest)

    def absorb_far(chunk, tile, newest):
        absorb(chunk, far_rows, tile, newest)
        close(chunk, finish_1)

    clear()

    def first_tiles(step, newest):
        chunk = 2 * step
        second = fill_near(chunk + 1, tile_b)
        absorb_near(chunk, tile_a, newest)
        third = fill_near(chunk + 2, tile_a)
        absorb_near(chunk + 1, tile_b, second)
        return third

    newest = lax.fori_loop(0, 2, first_tiles, fill_near(0, tile_a))
    further()
    second = fill_far(4, tile_b)
    absorb_near(4, tile_a, newest)
    newest = fill_far(3, tile_a)
    absorb_far(4, tile_b, second)
    second = fill_far(2, tile_b)
    absorb_far(3, tile_a, newest)
    newest = fill_far(1, tile_a)
    absorb_far(2, tile_b, second)
    for pair in (5, 6, 7):
        passes[pair].wait_recv()

    def last_tiles(step, newest):
        chunk = 5 + step
        second = fill_near(chunk, tile_b)
        absorb_far(jnp.where(step == 0, 1, chunk - 1), tile_a, newest)
        third = fill_far(chunk, tile_a)
        absorb_near(chunk, tile_b, second)
        return third

    newest = lax.fori_loop(0, 3, last_tiles, newest)
    second = fill_far(0, tile_b)
    absorb_far(7, tile_a, newest)
    absorb_far(0, tile_b, second)

    sent()
    for slot in range(1, group):
        part_1_copy(slot, along_q((8 - z_shift_of(slot // 2)) % 8, slot % 2)).wait()
    log_sum = combine(part_1)
    mass = spot_mass[...].reshape(1, width)
    log_count = math.log(256 * width)
    term = mass - log_sum + log_count
    spot_out[...] = (epsilon * (term + norms(spot_feat[...]))).reshape(width)
    dual[0:1, :] = term

    def dual_copy(slot):
        return pltpu.make_async_remote_copy(
            src_ref=dual.at[pl.ds(0, 1), :],
            dst_ref=dual.at[pl.ds(slot, 1), :],
            send_sem=dual_send.at[slot],
            recv_sem=dual_recv.at[slot],
            device_id=along_q(z_shift_of(slot // 2), slot % 2),
            device_id_type=MESH,
        )

    for slot in range(1, group):
        dual_copy(slot).start()
    for slot in range(1, group):
        dual_copy(slot).wait()
    values = dual[...]
    high = values.astype(jnp.bfloat16).astype(jnp.float32)
    middle = (values - high).astype(jnp.bfloat16).astype(jnp.float32)
    low = values - high - middle
    stacked = jnp.concatenate([high, middle, low, jnp.ones_like(low)], axis=0).astype(jnp.bfloat16)
    moved = dot_first(stacked, spread[...]).astype(jnp.bfloat16)
    for slot in range(group):
        at = slice(slot * width, (slot + 1) * width)
        spots[at, :] = spots[at, :] + moved[:, slot * depth:(slot + 1) * depth]

    def part_2_copy(slot, target):
        return pltpu.make_async_remote_copy(
            src_ref=out_2.at[slot],
            dst_ref=part_2.at[slot],
            send_sem=part_2_send.at[slot],
            recv_sem=part_2_recv.at[slot],
            device_id=target,
            device_id_type=MESH,
        )

    def owner(slot):
        i, j = lines_of(slot)
        return along_p((4 - shift(i)) % 4, (4 - shift(j)) % 4)

    def finish_2(chunk, top, sums):
        store_pair(out_2, 2 * chunk + 1, top, sums, width)
        if isinstance(chunk, int) and chunk == 0:
            store_pair(part_2, 0, top, sums, 0)
            part_2_copy(1, owner(1)).start()
        else:
            store_pair(out_2, 2 * chunk, top, sums, 0)
            part_2_copy(2 * chunk, owner(2 * chunk)).start()
            part_2_copy(2 * chunk + 1, owner(2 * chunk + 1)).start()

    clear()

    def fill_2(part, chunk, tile):
        return fill(spots, part * half_rows, half_rows, cells, chunk, tile)

    def both(step, newest):
        chunk = chunks - 1 - step
        second = fill_2(1, chunk, tile_b)
        absorb(chunk, half_rows, tile_a, newest)
        third = fill_2(0, chunk - 1, tile_a)
        absorb(chunk, half_rows, tile_b, second)
        close(chunk, finish_2)
        return third

    newest = lax.fori_loop(0, chunks - 1, both, fill_2(0, chunks - 1, tile_a))
    second = fill_2(1, 0, tile_b)
    absorb(0, half_rows, tile_a, newest)
    absorb(0, half_rows, tile_b, second)
    close(0, finish_2)
    for slot in range(1, group):
        part_2_copy(slot, owner(slot)).wait()
    log_sum = combine(part_2)
    mass = cell_mass[...].reshape(1, width)
    cell_out[...] = (epsilon * (mass - log_sum + norms(cell_feat[...]) + log_count)).reshape(width)


def local(*arguments):
    vmem = pl.BlockSpec(memory_space=pltpu.VMEM)
    points = group * width
    return pl.pallas_call(
        kernel,
        out_shape=[jax.ShapeDtypeStruct((width,), jnp.float32)] * 2,
        in_specs=[pl.BlockSpec(memory_space=pl.ANY)] * 7,
        out_specs=[vmem] * 2,
        scratch_shapes=[pltpu.VMEM(value.shape, value.dtype) for value in arguments]
        + [
            pltpu.SemaphoreType.DMA((7,)),
            pltpu.VMEM((points, depth), jnp.bfloat16),
            pltpu.VMEM((points, depth), jnp.bfloat16),
            pltpu.VMEM((4 * group, group * depth), jnp.bfloat16),
            pltpu.VMEM((far_rows, lanes), jnp.float32),
            pltpu.VMEM((far_rows, lanes), jnp.float32),
            pltpu.VMEM((chunks, 8, lanes), jnp.float32),
            pltpu.VMEM((chunks, 8, lanes), jnp.float32),
            pltpu.VMEM((group, 2, width), jnp.float32),
            pltpu.VMEM((group, 2, width), jnp.float32),
            pltpu.VMEM((group, width), jnp.float32),
            pltpu.VMEM((group, 2, width), jnp.float32),
            pltpu.VMEM((group, 2, width), jnp.float32),
        ]
        + [pltpu.SemaphoreType.DMA((count,)) for count in (17, 17, 25, 25)]
        + [pltpu.SemaphoreType.DMA((group,))] * 6,
        compiler_params=pltpu.CompilerParams(
            collective_id=0, has_side_effects=True, vmem_limit_bytes=56 * 1024 * 1024
        ),
        name="sweep",
    )(*arguments)


def solution(mesh):
    column = P(None, ("blk", "grp"))
    flat = P(("blk", "grp"))
    return jax.shard_map(
        local,
        mesh=mesh,
        in_specs=(column, column, flat, column, column, flat, flat),
        out_specs=(flat, flat),
        check_vma=False,
    )
```

```python
import math

import jax
import jax.numpy as jnp
from jax import lax
from jax.experimental import pallas as pl
from jax.experimental.pallas import tpu as pltpu
from jax.sharding import PartitionSpec as P

epsilon = 0.25
width = 192
depth = 128
features, factors = 64, 34
offset_lane = features + factors
dual_lane = offset_lane + 3
group = 16
lanes = 384
chunks = group * width // lanes
near_rows = 7 * width
far_rows = 9 * width
half_rows = group * width // 2
part_rows = width // 2
lowest = -1e30
MESH = pl.DeviceIdType.MESH


def dot_first(left, right):
    return lax.dot_general(
        left, right, (((0,), (0,)), ((), ())), preferred_element_type=jnp.float32
    )


def dot_last(left, right):
    return lax.dot_general(
        left, right, (((1,), (1,)), ((), ())), preferred_element_type=jnp.float32
    )


def placing(count, first_lane, scale):
    source = lax.broadcasted_iota(jnp.int32, (count, depth), 0)
    lane = lax.broadcasted_iota(jnp.int32, (count, depth), 1)
    return jnp.where(lane == source + first_lane, scale, 0.0).astype(jnp.bfloat16)


def pieces(row):
    high = row.astype(jnp.bfloat16).astype(jnp.float32)
    rest = row - high
    middle = rest.astype(jnp.bfloat16).astype(jnp.float32)
    low = rest - middle
    at = lax.broadcasted_iota(jnp.int32, (16, row.shape[1]), 0)
    stacked = jnp.where(at == 0, high, jnp.where(at == 1, middle, jnp.where(at == 2, low, 0.0)))
    return stacked.astype(jnp.bfloat16)


def lane_between(first, last):
    lane = lax.broadcasted_iota(jnp.int32, (width, depth), 1)
    return (lane >= first) & (lane < last)


def norms(feat):
    values = feat.astype(jnp.float32)
    return jnp.sum(values * values, axis=0, keepdims=True) * (1.0 / (features * epsilon))


def z_shift(pair):
    return jnp.where(pair % 2 == 1, (pair + 1) // 2, (8 - pair // 2) % 8)


def z_shift_of(pair):
    return (pair + 1) // 2 if pair % 2 else (8 - pair // 2) % 8


def shift(place):
    return place + (place // 2) * (5 - 2 * place)


def slot_of(i, j):
    if j == 0:
        return i
    return 3 + j if i == 0 else 7 + 3 * (j - 1) + i - 1


def lines_of(slot):
    i = jnp.where(slot < 4, slot, jnp.where(slot < 7, 0, 1 + (slot + 2) % 3))
    j = jnp.where(slot < 4, 0, jnp.where(slot < 7, slot - 3, 1 + (slot - 7) // 3))
    return i, j


def kernel(
    spot_feat_in, spot_fac_in, spot_mass_in, cell_feat_in, cell_fac_in, cell_mass_in, cell_pot_in,
    spot_out, cell_out,
    spot_feat, spot_fac, spot_mass, cell_feat, cell_fac, cell_mass, cell_pot, input_sem,
    spots, cells, spread, tile_a, tile_b, highest, total,
    part_1, out_1, dual, part_2, out_2,
    spot_send, spot_recv, cell_send, cell_recv,
    part_1_send, part_1_recv, dual_send, dual_recv, part_2_send, part_2_recv,
):
    blk, grp = lax.axis_index("blk"), lax.axis_index("grp")
    my_x, my_y = (blk // 4) * 2 + grp // 16, blk % 4
    my_z, my_core = (grp % 16) // 2, grp % 2

    def place(x, y, z, core):
        return ((x // 2) * 4 + y, (x % 2) * 16 + z * 2 + core)

    def along_q(shift, other):
        return place(my_x, my_y, (my_z + shift) % 8, (my_core + other) % 2)

    def along_p(dx, dy):
        return place((my_x + dx) % 4, (my_y + dy) % 4, my_z, my_core)

    loads = [
        pltpu.make_async_copy(source, target, input_sem.at[at])
        for at, (source, target) in enumerate((
            (cell_feat_in, cell_feat), (cell_fac_in, cell_fac), (cell_pot_in, cell_pot),
            (spot_feat_in, spot_feat), (spot_fac_in, spot_fac),
            (spot_mass_in, spot_mass), (cell_mass_in, cell_mass),
        ))
    ]
    for load in loads:
        load.start()

    barrier = pltpu.get_barrier_semaphore()
    line = (1, 2, 3)
    partners = (
        [along_q(0, 1)]
        + [along_q(z_shift_of(pair), 0) for pair in range(1, 5)]
        + [along_p(shift(i), 0) for i in line]
        + [along_p(0, shift(j)) for j in line]
    )
    for partner in partners:
        pl.semaphore_signal(barrier, inc=1, device_id=partner, device_id_type=MESH)
    for load in loads:
        load.wait()

    own_spots = (
        dot_first(spot_feat[...], placing(features, 0, 0.125))
        + dot_first(spot_fac[...], placing(factors, features, -4.0))
    )
    own_spots = jnp.where(lane_between(offset_lane, offset_lane + 3), 1.0, own_spots)
    spots[0:width, :] = own_spots.astype(jnp.bfloat16)
    cell_norm = norms(cell_feat[...])
    potential = cell_pot[...].reshape(1, width) * (1.0 / epsilon)
    own_cells = (
        dot_first(cell_feat[...], placing(features, 0, 1.0))
        + dot_first(cell_fac[...], placing(factors, features, 1.0))
        + dot_first(pieces(potential - cell_norm), placing(16, offset_lane, 1.0))
    )
    own_cells = jnp.where(lane_between(dual_lane, dual_lane + 3), 1.0, own_cells)
    cells[0:width, :] = own_cells.astype(jnp.bfloat16)

    source = lax.broadcasted_iota(jnp.int32, spread.shape, 0)
    target = lax.broadcasted_iota(jnp.int32, spread.shape, 1)
    lane, kind = target % depth, source // 8
    value = jnp.where(
        lane == dual_lane + kind,
        jnp.where(kind < 3, 1.0, 0.0),
        jnp.where((kind == 3) & (lane >= offset_lane) & (lane < dual_lane), -1.0, 0.0),
    )
    spread[...] = jnp.where(target // depth == source % 8, value, 0.0).astype(jnp.bfloat16)

    pl.semaphore_wait(barrier, len(partners))

    def spot_copy(pair, source=0, first=0, count=width, flight=None):
        target = z_shift_of(pair) - z_shift_of(source)
        at = 2 * pair if flight is None else flight
        return pltpu.make_async_remote_copy(
            src_ref=spots.at[pl.ds(2 * source * width + first, count), :],
            dst_ref=spots.at[pl.ds(2 * pair * width + first, count), :],
            send_sem=spot_send.at[at],
            recv_sem=spot_recv.at[at],
            device_id=along_q((target + 8) % 8, 0),
            device_id_type=MESH,
        )

    def spot_pass(pair):
        return pltpu.make_async_remote_copy(
            src_ref=spots.at[pl.ds(2 * pair * width, width), :],
            dst_ref=spots.at[pl.ds((2 * pair + 1) * width, width), :],
            send_sem=spot_send.at[2 * pair + 1],
            recv_sem=spot_recv.at[2 * pair + 1],
            device_id=along_q(0, 1),
            device_id_type=MESH,
        )

    def cell_copy(i, j):
        slot = slot_of(i, j)
        return pltpu.make_async_remote_copy(
            src_ref=cells.at[pl.ds(0, width), :],
            dst_ref=cells.at[pl.ds(slot * width, width), :],
            send_sem=cell_send.at[slot],
            recv_sem=cell_recv.at[slot],
            device_id=along_p(shift(i), shift(j)),
            device_id_type=MESH,
        )

    def cell_turn(i, j, along_y):
        source, first = (slot_of(i, 0), 0) if along_y else (slot_of(0, j), part_rows)
        at = slot_of(i, j) + (0 if along_y else 9)
        return pltpu.make_async_remote_copy(
            src_ref=cells.at[pl.ds(source * width + first, part_rows), :],
            dst_ref=cells.at[pl.ds(slot_of(i, j) * width + first, part_rows), :],
            send_sem=cell_send.at[at],
            recv_sem=cell_recv.at[at],
            device_id=along_p(0, shift(j)) if along_y else along_p(shift(i), 0),
            device_id_type=MESH,
        )

    spot_direct = [spot_copy(pair) for pair in (3, 4, 1, 2)]
    spot_further = [
        spot_copy(5, 3),
        spot_copy(6, 4),
        spot_copy(7, 3, 0, part_rows),
        spot_copy(7, 4, part_rows, part_rows, 16),
    ]
    cell_direct = [cell_copy(0, j) for j in line] + [cell_copy(i, 0) for i in line]
    cell_turns = [
        cell_turn(i, j, along_y) for i in line for j in line for along_y in (True, False)
    ]
    passes = [spot_pass(pair) for pair in range(8)]
    passes[0].start()
    for spot_step, cell_step in zip(spot_direct, ((0, 3), (1, 4), (2,), (5,))):
        spot_step.start()
        for at in cell_step:
            cell_direct[at].start()
    for i in line:
        cell_copy(i, 0).wait_recv()
        for j in line:
            cell_turn(i, j, True).start()
        cell_copy(0, i).wait_recv()
        for j in line:
            cell_turn(j, i, False).start()
    for pair in (1, 2):
        spot_copy(pair).wait_recv()
        passes[pair].start()
    for pair in (3, 4):
        spot_copy(pair).wait_recv()
    for step in spot_further:
        step.start()
    for pair in (3, 4):
        passes[pair].start()
    passes[0].wait_recv()

    def further():
        for step in spot_further:
            step.wait_recv()
        for pair in (5, 6, 7):
            passes[pair].start()
        for step in cell_turns:
            step.wait_recv()

    def sent():
        for step in spot_direct + spot_further + cell_direct + cell_turns + passes:
            step.wait_send()

    def clear():
        highest[...] = jnp.full(highest.shape, lowest, jnp.float32)
        total[...] = jnp.zeros(total.shape, jnp.float32)

    def fill(by_row, first, count, by_lane, chunk, tile):
        right = by_lane[pl.ds(pl.multiple_of(chunk * lanes, lanes), lanes), :]
        scores = dot_last(by_row[pl.ds(first, count), :], right)
        tile[0:count, :] = scores
        return jnp.max(scores.reshape(count // 8, 8, lanes), axis=0)

    def absorb(chunk, count, tile, newest):
        before = highest[chunk]
        after = jnp.maximum(before, newest)
        highest[chunk] = after
        scores = tile[0:count, :].reshape(count // 8, 8, lanes)
        total[chunk] = total[chunk] * jnp.exp(before - after) + jnp.sum(
            jnp.exp(scores - after[None]), axis=0
        )

    def close(chunk, finish):
        top = jnp.max(highest[chunk], axis=0, keepdims=True)
        sums = jnp.sum(total[chunk] * jnp.exp(highest[chunk] - top), axis=0, keepdims=True)
        finish(chunk, top, sums)

    def store_pair(out, slot, top, sums, first):
        out[slot, 0:1, 0:width] = top[:, first:first + width]
        out[slot, 1:2, 0:width] = sums[:, first:first + width]

    def combine(part):
        top = part[0, 0:1, 0:width]
        for slot in range(1, group):
            top = jnp.maximum(top, part[slot, 0:1, 0:width])
        sums = jnp.zeros_like(top)
        for slot in range(group):
            sums += part[slot, 1:2, 0:width] * jnp.exp(part[slot, 0:1, 0:width] - top)
        return top + jnp.log(sums)

    def part_1_copy(slot, target):
        return pltpu.make_async_remote_copy(
            src_ref=out_1.at[slot],
            dst_ref=part_1.at[slot],
            send_sem=part_1_send.at[slot],
            recv_sem=part_1_recv.at[slot],
            device_id=target,
            device_id_type=MESH,
        )

    def finish_1(chunk, top, sums):
        store_pair(out_1, 2 * chunk + 1, top, sums, width)
        if isinstance(chunk, int) and chunk == 0:
            store_pair(part_1, 0, top, sums, 0)
            part_1_copy(1, along_q(0, 1)).start()
        else:
            store_pair(out_1, 2 * chunk, top, sums, 0)
            back = (8 - z_shift(chunk)) % 8
            part_1_copy(2 * chunk, along_q(back, 0)).start()
            part_1_copy(2 * chunk + 1, along_q(back, 1)).start()

    def fill_near(chunk, tile):
        return fill(cells, 0, near_rows, spots, chunk, tile)

    def fill_far(chunk, tile):
        return fill(cells, near_rows, far_rows, spots, chunk, tile)

    def absorb_near(chunk, tile, newest):
        absorb(chunk, near_rows, tile, newest)

    def absorb_far(chunk, tile, newest):
        absorb(chunk, far_rows, tile, newest)
        close(chunk, finish_1)

    clear()

    def first_tiles(step, newest):
        chunk = 2 * step
        spot_pass(chunk + 1).wait_recv()
        spot_pass(chunk + 2).wait_recv()
        second = fill_near(chunk + 1, tile_b)
        absorb_near(chunk, tile_a, newest)
        third = fill_near(chunk + 2, tile_a)
        absorb_near(chunk + 1, tile_b, second)
        return third

    newest = lax.fori_loop(0, 2, first_tiles, fill_near(0, tile_a))
    further()
    second = fill_far(4, tile_b)
    absorb_near(4, tile_a, newest)
    newest = fill_far(3, tile_a)
    absorb_far(4, tile_b, second)
    for pair in (5, 6, 7):
        passes[pair].wait_recv()

    def last_tiles(step, newest):
        chunk = 7 - step
        second = fill_near(chunk, tile_b)
        absorb_far(jnp.where(step == 0, 3, chunk + 1), tile_a, newest)
        third = fill_far(chunk, tile_a)
        absorb_near(chunk, tile_b, second)
        return third

    newest = lax.fori_loop(0, 3, last_tiles, newest)
    second = fill_far(2, tile_b)
    absorb_far(5, tile_a, newest)
    newest = fill_far(1, tile_a)
    absorb_far(2, tile_b, second)
    second = fill_far(0, tile_b)
    absorb_far(1, tile_a, newest)
    absorb_far(0, tile_b, second)

    sent()
    for slot in range(1, group):
        part_1_copy(slot, along_q((8 - z_shift_of(slot // 2)) % 8, slot % 2)).wait()
    log_sum = combine(part_1)
    mass = spot_mass[...].reshape(1, width)
    log_count = math.log(256 * width)
    term = mass - log_sum + log_count
    spot_out[...] = (epsilon * (term + norms(spot_feat[...]))).reshape(width)
    dual[0:1, :] = term

    def dual_copy(slot):
        return pltpu.make_async_remote_copy(
            src_ref=dual.at[pl.ds(0, 1), :],
            dst_ref=dual.at[pl.ds(slot, 1), :],
            send_sem=dual_send.at[slot],
            recv_sem=dual_recv.at[slot],
            device_id=along_q(z_shift_of(slot // 2), slot % 2),
            device_id_type=MESH,
        )

    for slot in range(group - 1, 0, -1):
        dual_copy(slot).start()

    def take_terms(part):
        values = dual[8 * part:8 * part + 8, :]
        high = values.astype(jnp.bfloat16).astype(jnp.float32)
        middle = (values - high).astype(jnp.bfloat16).astype(jnp.float32)
        low = values - high - middle
        stacked = jnp.concatenate([high, middle, low, jnp.ones_like(low)], axis=0)
        moved = dot_first(stacked.astype(jnp.bfloat16), spread[...]).astype(jnp.bfloat16)
        for at in range(8):
            own = slice((8 * part + at) * width, (8 * part + at + 1) * width)
            spots[own, :] = spots[own, :] + moved[:, at * depth:(at + 1) * depth]

    for slot in range(1, 8):
        dual_copy(slot).wait()
    take_terms(0)

    def part_2_copy(slot, target):
        return pltpu.make_async_remote_copy(
            src_ref=out_2.at[slot],
            dst_ref=part_2.at[slot],
            send_sem=part_2_send.at[slot],
            recv_sem=part_2_recv.at[slot],
            device_id=target,
            device_id_type=MESH,
        )

    def owner(slot):
        i, j = lines_of(slot)
        return along_p((4 - shift(i)) % 4, (4 - shift(j)) % 4)

    def finish_2(chunk, top, sums):
        store_pair(out_2, 2 * chunk + 1, top, sums, width)
        if isinstance(chunk, int) and chunk == 0:
            store_pair(part_2, 0, top, sums, 0)
            part_2_copy(1, owner(1)).start()
        else:
            store_pair(out_2, 2 * chunk, top, sums, 0)
            part_2_copy(2 * chunk, owner(2 * chunk)).start()
            part_2_copy(2 * chunk + 1, owner(2 * chunk + 1)).start()

    clear()

    def fill_2(part, chunk, tile):
        return fill(spots, part * half_rows, half_rows, cells, chunk, tile)

    def both(step, newest):
        chunk = chunks - 1 - step
        second = fill_2(1, chunk, tile_b)
        absorb(chunk, half_rows, tile_a, newest)
        third = fill_2(0, chunk - 1, tile_a)
        absorb(chunk, half_rows, tile_b, second)
        close(chunk, finish_2)
        return third

    newest = fill_2(0, chunks - 1, tile_a)
    for slot in range(8, group):
        dual_copy(slot).wait()
    take_terms(1)
    newest = lax.fori_loop(0, chunks - 1, both, newest)
    second = fill_2(1, 0, tile_b)
    absorb(0, half_rows, tile_a, newest)
    absorb(0, half_rows, tile_b, second)
    close(0, finish_2)
    for slot in range(1, group):
        part_2_copy(slot, owner(slot)).wait()
    log_sum = combine(part_2)
    mass = cell_mass[...].reshape(1, width)
    cell_out[...] = (epsilon * (mass - log_sum + norms(cell_feat[...]) + log_count)).reshape(width)


def local(*arguments):
    vmem = pl.BlockSpec(memory_space=pltpu.VMEM)
    points = group * width
    return pl.pallas_call(
        kernel,
        out_shape=[jax.ShapeDtypeStruct((width,), jnp.float32)] * 2,
        in_specs=[pl.BlockSpec(memory_space=pl.ANY)] * 7,
        out_specs=[vmem] * 2,
        scratch_shapes=[pltpu.VMEM(value.shape, value.dtype) for value in arguments]
        + [
            pltpu.SemaphoreType.DMA((7,)),
            pltpu.VMEM((points, depth), jnp.bfloat16),
            pltpu.VMEM((points, depth), jnp.bfloat16),
            pltpu.VMEM((4 * 8, 8 * depth), jnp.bfloat16),
            pltpu.VMEM((far_rows, lanes), jnp.float32),
            pltpu.VMEM((far_rows, lanes), jnp.float32),
            pltpu.VMEM((chunks, 8, lanes), jnp.float32),
            pltpu.VMEM((chunks, 8, lanes), jnp.float32),
            pltpu.VMEM((group, 2, width), jnp.float32),
            pltpu.VMEM((group, 2, width), jnp.float32),
            pltpu.VMEM((group, width), jnp.float32),
            pltpu.VMEM((group, 2, width), jnp.float32),
            pltpu.VMEM((group, 2, width), jnp.float32),
        ]
        + [pltpu.SemaphoreType.DMA((count,)) for count in (17, 17, 25, 25)]
        + [pltpu.SemaphoreType.DMA((group,))] * 6,
        compiler_params=pltpu.CompilerParams(
            collective_id=0, has_side_effects=True, vmem_limit_bytes=56 * 1024 * 1024
        ),
        name="sweep",
    )(*arguments)


def solution(mesh):
    column = P(None, ("blk", "grp"))
    flat = P(("blk", "grp"))
    return jax.shard_map(
        local,
        mesh=mesh,
        in_specs=(column, column, flat, column, column, flat, flat),
        out_specs=(flat, flat),
        check_vma=False,
    )
```

```python
import math

import jax
import jax.numpy as jnp
from jax import lax
from jax.experimental import pallas as pl
from jax.experimental.pallas import tpu as pltpu
from jax.sharding import PartitionSpec as P

epsilon = 0.25
width = 192
depth = 128
features, factors = 64, 34
offset_lane = features + factors
dual_lane = offset_lane + 3
group = 16
lanes = 768
per_chunk = lanes // width
chunks = group * width // lanes
near_rows = 7 * width
far_rows = 9 * width
near_part, far_part, even_part = near_rows // 4, far_rows // 4, group * width // 8
part_rows = width // 2
lowest = -1e30
MESH = pl.DeviceIdType.MESH


def dot_first(left, right):
    return lax.dot_general(
        left, right, (((0,), (0,)), ((), ())), preferred_element_type=jnp.float32
    )


def dot_last(left, right):
    return lax.dot_general(
        left, right, (((1,), (1,)), ((), ())), preferred_element_type=jnp.float32
    )


def placing(count, first_lane, scale):
    source = lax.broadcasted_iota(jnp.int32, (count, depth), 0)
    lane = lax.broadcasted_iota(jnp.int32, (count, depth), 1)
    return jnp.where(lane == source + first_lane, scale, 0.0).astype(jnp.bfloat16)


def pieces(row):
    high = row.astype(jnp.bfloat16).astype(jnp.float32)
    rest = row - high
    middle = rest.astype(jnp.bfloat16).astype(jnp.float32)
    low = rest - middle
    at = lax.broadcasted_iota(jnp.int32, (16, row.shape[1]), 0)
    stacked = jnp.where(at == 0, high, jnp.where(at == 1, middle, jnp.where(at == 2, low, 0.0)))
    return stacked.astype(jnp.bfloat16)


def lane_between(first, last):
    lane = lax.broadcasted_iota(jnp.int32, (width, depth), 1)
    return (lane >= first) & (lane < last)


def norms(feat):
    values = feat.astype(jnp.float32)
    return jnp.sum(values * values, axis=0, keepdims=True) * (1.0 / (features * epsilon))


def z_shift(pair):
    return jnp.where(pair % 2 == 1, (pair + 1) // 2, (8 - pair // 2) % 8)


def z_shift_of(pair):
    return (pair + 1) // 2 if pair % 2 else (8 - pair // 2) % 8


def shift(place):
    return place + (place // 2) * (5 - 2 * place)


def slot_of(i, j):
    if j == 0:
        return i
    return 3 + j if i == 0 else 7 + 3 * (j - 1) + i - 1


def lines_of(slot):
    i = jnp.where(slot < 4, slot, jnp.where(slot < 7, 0, 1 + (slot + 2) % 3))
    j = jnp.where(slot < 4, 0, jnp.where(slot < 7, slot - 3, 1 + (slot - 7) // 3))
    return i, j


def kernel(
    spot_feat_in, spot_fac_in, spot_mass_in, cell_feat_in, cell_fac_in, cell_mass_in, cell_pot_in,
    spot_out, cell_out,
    spot_feat, spot_fac, spot_mass, cell_feat, cell_fac, cell_mass, cell_pot, input_sem,
    spots, cells, spread, tile_a, tile_b, highest, total,
    part_1, out_1, dual, part_2, out_2,
    spot_send, spot_recv, cell_send, cell_recv,
    part_1_send, part_1_recv, dual_send, dual_recv, part_2_send, part_2_recv,
):
    blk, grp = lax.axis_index("blk"), lax.axis_index("grp")
    my_x, my_y = (blk // 4) * 2 + grp // 16, blk % 4
    my_z, my_core = (grp % 16) // 2, grp % 2

    def place(x, y, z, core):
        return ((x // 2) * 4 + y, (x % 2) * 16 + z * 2 + core)

    def along_q(shift, other):
        return place(my_x, my_y, (my_z + shift) % 8, (my_core + other) % 2)

    def along_p(dx, dy):
        return place((my_x + dx) % 4, (my_y + dy) % 4, my_z, my_core)

    loads = [
        pltpu.make_async_copy(source, target, input_sem.at[at])
        for at, (source, target) in enumerate((
            (cell_feat_in, cell_feat), (cell_fac_in, cell_fac), (cell_pot_in, cell_pot),
            (spot_feat_in, spot_feat), (spot_fac_in, spot_fac),
            (spot_mass_in, spot_mass), (cell_mass_in, cell_mass),
        ))
    ]
    for load in loads:
        load.start()

    barrier = pltpu.get_barrier_semaphore()
    line = (1, 2, 3)
    partners = (
        [along_q(0, 1)]
        + [along_q(z_shift_of(pair), 0) for pair in range(1, 5)]
        + [along_p(shift(i), 0) for i in line]
        + [along_p(0, shift(j)) for j in line]
    )
    for partner in partners:
        pl.semaphore_signal(barrier, inc=1, device_id=partner, device_id_type=MESH)
    for load in loads:
        load.wait()

    own_spots = (
        dot_first(spot_feat[...], placing(features, 0, 0.125))
        + dot_first(spot_fac[...], placing(factors, features, -4.0))
    )
    own_spots = jnp.where(lane_between(offset_lane, offset_lane + 3), 1.0, own_spots)
    spots[0:width, :] = own_spots.astype(jnp.bfloat16)
    cell_norm = norms(cell_feat[...])
    potential = cell_pot[...].reshape(1, width) * (1.0 / epsilon)
    own_cells = (
        dot_first(cell_feat[...], placing(features, 0, 1.0))
        + dot_first(cell_fac[...], placing(factors, features, 1.0))
        + dot_first(pieces(potential - cell_norm), placing(16, offset_lane, 1.0))
    )
    own_cells = jnp.where(lane_between(dual_lane, dual_lane + 3), 1.0, own_cells)
    cells[0:width, :] = own_cells.astype(jnp.bfloat16)

    source = lax.broadcasted_iota(jnp.int32, spread.shape, 0)
    target = lax.broadcasted_iota(jnp.int32, spread.shape, 1)
    lane, kind = target % depth, source // 8
    value = jnp.where(
        lane == dual_lane + kind,
        jnp.where(kind < 3, 1.0, 0.0),
        jnp.where((kind == 3) & (lane >= offset_lane) & (lane < dual_lane), -1.0, 0.0),
    )
    spread[...] = jnp.where(target // depth == source % 8, value, 0.0).astype(jnp.bfloat16)

    pl.semaphore_wait(barrier, len(partners))

    def spot_copy(pair, source=0, first=0, count=width, flight=None):
        target = z_shift_of(pair) - z_shift_of(source)
        at = 2 * pair if flight is None else flight
        return pltpu.make_async_remote_copy(
            src_ref=spots.at[pl.ds(2 * source * width + first, count), :],
            dst_ref=spots.at[pl.ds(2 * pair * width + first, count), :],
            send_sem=spot_send.at[at],
            recv_sem=spot_recv.at[at],
            device_id=along_q((target + 8) % 8, 0),
            device_id_type=MESH,
        )

    def spot_pass(pair):
        return pltpu.make_async_remote_copy(
            src_ref=spots.at[pl.ds(2 * pair * width, width), :],
            dst_ref=spots.at[pl.ds((2 * pair + 1) * width, width), :],
            send_sem=spot_send.at[2 * pair + 1],
            recv_sem=spot_recv.at[2 * pair + 1],
            device_id=along_q(0, 1),
            device_id_type=MESH,
        )

    def cell_copy(i, j):
        slot = slot_of(i, j)
        return pltpu.make_async_remote_copy(
            src_ref=cells.at[pl.ds(0, width), :],
            dst_ref=cells.at[pl.ds(slot * width, width), :],
            send_sem=cell_send.at[slot],
            recv_sem=cell_recv.at[slot],
            device_id=along_p(shift(i), shift(j)),
            device_id_type=MESH,
        )

    def cell_turn(i, j, along_y):
        source, first = (slot_of(i, 0), 0) if along_y else (slot_of(0, j), part_rows)
        at = slot_of(i, j) + (0 if along_y else 9)
        return pltpu.make_async_remote_copy(
            src_ref=cells.at[pl.ds(source * width + first, part_rows), :],
            dst_ref=cells.at[pl.ds(slot_of(i, j) * width + first, part_rows), :],
            send_sem=cell_send.at[at],
            recv_sem=cell_recv.at[at],
            device_id=along_p(0, shift(j)) if along_y else along_p(shift(i), 0),
            device_id_type=MESH,
        )

    spot_direct = [spot_copy(pair) for pair in (3, 4, 1, 2)]
    spot_further = [
        spot_copy(5, 3),
        spot_copy(6, 4),
        spot_copy(7, 3, 0, part_rows),
        spot_copy(7, 4, part_rows, part_rows, 16),
    ]
    cell_direct = [cell_copy(0, j) for j in line] + [cell_copy(i, 0) for i in line]
    cell_turns = [
        cell_turn(i, j, along_y) for i in line for j in line for along_y in (True, False)
    ]
    passes = [spot_pass(pair) for pair in range(8)]
    passes[0].start()
    for spot_step, cell_step in zip(spot_direct, ((0, 3), (1, 4), (2,), (5,))):
        spot_step.start()
        for at in cell_step:
            cell_direct[at].start()
    for i in line:
        cell_copy(i, 0).wait_recv()
        for j in line:
            cell_turn(i, j, True).start()
        cell_copy(0, i).wait_recv()
        for j in line:
            cell_turn(j, i, False).start()
    for pair in (1, 2):
        spot_copy(pair).wait_recv()
        passes[pair].start()
    for pair in (3, 4):
        spot_copy(pair).wait_recv()
    for step in spot_further:
        step.start()
    for pair in (3, 4):
        passes[pair].start()
    passes[0].wait_recv()

    def further():
        for step in spot_further:
            step.wait_recv()
        for pair in (5, 6, 7):
            passes[pair].start()
        for step in cell_turns:
            step.wait_recv()

    def sent():
        for step in spot_direct + spot_further + cell_direct + cell_turns + passes:
            step.wait_send()

    def clear():
        highest[...] = jnp.full(highest.shape, lowest, jnp.float32)
        total[...] = jnp.zeros(total.shape, jnp.float32)

    def fill(by_row, first, count, by_lane, chunk, tile):
        right = by_lane[pl.ds(pl.multiple_of(chunk * lanes, lanes), lanes), :]
        scores = dot_last(by_row[pl.ds(first, count), :], right)
        tile[0:count, :] = scores
        return jnp.max(scores.reshape(count // 8, 8, lanes), axis=0)

    def absorb(chunk, count, tile, newest):
        before = highest[chunk]
        after = jnp.maximum(before, newest)
        highest[chunk] = after
        scores = tile[0:count, :].reshape(count // 8, 8, lanes)
        total[chunk] = total[chunk] * jnp.exp(before - after) + jnp.sum(
            jnp.exp(scores - after[None]), axis=0
        )

    def through(jobs, pending):
        for job in jobs:
            by_row, first, count, by_lane, chunk = job
            tile = tile_a if pending is None else pending[3]
            newest = fill(by_row, first, count, by_lane, chunk, tile)
            if pending is not None:
                absorb(*pending[:2], pending[2], pending[4])
            pending = (chunk, count, tile, tile_b if tile is tile_a else tile_a, newest)
        return pending

    def close(chunk, finish):
        top = jnp.max(highest[chunk], axis=0, keepdims=True)
        sums = jnp.sum(total[chunk] * jnp.exp(highest[chunk] - top), axis=0, keepdims=True)
        finish(chunk, top, sums)

    def store_pair(out, slot, top, sums, at):
        out[slot, 0:1, :] = top[:, at * width:(at + 1) * width]
        out[slot, 1:2, :] = sums[:, at * width:(at + 1) * width]

    def combine(part):
        top = part[0, 0:1, 0:width]
        for slot in range(1, group):
            top = jnp.maximum(top, part[slot, 0:1, 0:width])
        sums = jnp.zeros_like(top)
        for slot in range(group):
            sums += part[slot, 1:2, 0:width] * jnp.exp(part[slot, 0:1, 0:width] - top)
        return top + jnp.log(sums)

    def part_1_copy(slot, target):
        return pltpu.make_async_remote_copy(
            src_ref=out_1.at[slot],
            dst_ref=part_1.at[slot],
            send_sem=part_1_send.at[slot],
            recv_sem=part_1_recv.at[slot],
            device_id=target,
            device_id_type=MESH,
        )

    def finish_1(chunk, top, sums):
        last = isinstance(chunk, int)
        if last:
            store_pair(part_1, 0, top, sums, 0)
        for at in range(last, per_chunk):
            slot = per_chunk * chunk + at
            store_pair(out_1, slot, top, sums, at)
            back = (8 - z_shift(slot // 2)) % 8
            part_1_copy(slot, along_q(back, at % 2)).start()

    def near_jobs(chunk):
        return [(cells, part * near_part, near_part, spots, chunk) for part in range(4)]

    def far_jobs(chunk):
        return [(cells, near_rows + part * far_part, far_part, spots, chunk) for part in range(4)]

    def rest(pending):
        return pending[0], pending[1], pending[2], pending[4]

    clear()
    passes[1].wait_recv()
    pending = through(near_jobs(0), None)
    for pair in (2, 3):
        passes[pair].wait_recv()
    pending = through(near_jobs(1), pending)
    further()
    passes[4].wait_recv()
    pending = through(far_jobs(1), pending)
    for pair in (5, 6, 7):
        passes[pair].wait_recv()

    def last_tiles(step, newest):
        chunk = 3 - step
        before = jnp.where(step == 0, 1, chunk + 1)
        held = (before, far_part, tile_b, tile_a, newest)
        held = through(near_jobs(chunk)[:1], held)
        close(before, finish_1)
        held = through(near_jobs(chunk)[1:] + far_jobs(chunk), held)
        return held[4]

    newest = lax.fori_loop(0, 2, last_tiles, pending[4])
    pending = through(far_jobs(0)[:1], (2, far_part, tile_b, tile_a, newest))
    close(jnp.int32(2), finish_1)
    pending = through(far_jobs(0)[1:], pending)
    absorb(*rest(pending))
    close(0, finish_1)

    sent()
    for slot in range(1, group):
        part_1_copy(slot, along_q((8 - z_shift_of(slot // 2)) % 8, slot % 2)).wait()
    log_sum = combine(part_1)
    mass = spot_mass[...].reshape(1, width)
    log_count = math.log(256 * width)
    term = mass - log_sum + log_count
    spot_out[...] = (epsilon * (term + norms(spot_feat[...]))).reshape(width)
    dual[0:1, :] = term

    def dual_copy(slot):
        return pltpu.make_async_remote_copy(
            src_ref=dual.at[pl.ds(0, 1), :],
            dst_ref=dual.at[pl.ds(slot, 1), :],
            send_sem=dual_send.at[slot],
            recv_sem=dual_recv.at[slot],
            device_id=along_q(z_shift_of(slot // 2), slot % 2),
            device_id_type=MESH,
        )

    for slot in range(group - 1, 0, -1):
        dual_copy(slot).start()

    def take_terms(part):
        values = dual[8 * part:8 * part + 8, :]
        high = values.astype(jnp.bfloat16).astype(jnp.float32)
        middle = (values - high).astype(jnp.bfloat16).astype(jnp.float32)
        low = values - high - middle
        stacked = jnp.concatenate([high, middle, low, jnp.ones_like(low)], axis=0)
        moved = dot_first(stacked.astype(jnp.bfloat16), spread[...]).astype(jnp.bfloat16)
        for at in range(8):
            own = slice((8 * part + at) * width, (8 * part + at + 1) * width)
            spots[own, :] = spots[own, :] + moved[:, at * depth:(at + 1) * depth]

    for slot in range(1, 8):
        dual_copy(slot).wait()
    take_terms(0)

    def part_2_copy(slot, target):
        return pltpu.make_async_remote_copy(
            src_ref=out_2.at[slot],
            dst_ref=part_2.at[slot],
            send_sem=part_2_send.at[slot],
            recv_sem=part_2_recv.at[slot],
            device_id=target,
            device_id_type=MESH,
        )

    def owner(slot):
        i, j = lines_of(slot)
        return along_p((4 - shift(i)) % 4, (4 - shift(j)) % 4)

    def finish_2(chunk, top, sums):
        last = isinstance(chunk, int)
        if last:
            store_pair(part_2, 0, top, sums, 0)
        for at in range(last, per_chunk):
            slot = per_chunk * chunk + at
            store_pair(out_2, slot, top, sums, at)
            part_2_copy(slot, owner(slot)).start()

    def even_jobs(chunk):
        return [(spots, part * even_part, even_part, cells, chunk) for part in range(8)]

    clear()
    top_chunk = chunks - 1
    pending = through(even_jobs(top_chunk)[:4], None)
    for slot in range(8, group):
        dual_copy(slot).wait()
    take_terms(1)
    pending = through(even_jobs(top_chunk)[4:], pending)

    def next_chunk(step, newest):
        chunk = chunks - 2 - step
        held = (chunk + 1, even_part, tile_b, tile_a, newest)
        held = through(even_jobs(chunk)[:1], held)
        close(chunk + 1, finish_2)
        return through(even_jobs(chunk)[1:], held)[4]

    newest = lax.fori_loop(0, chunks - 1, next_chunk, pending[4])
    absorb(0, even_part, tile_b, newest)
    close(0, finish_2)
    for slot in range(1, group):
        part_2_copy(slot, owner(slot)).wait()
    log_sum = combine(part_2)
    mass = cell_mass[...].reshape(1, width)
    cell_out[...] = (epsilon * (mass - log_sum + norms(cell_feat[...]) + log_count)).reshape(width)


def local(*arguments):
    vmem = pl.BlockSpec(memory_space=pltpu.VMEM)
    points = group * width
    return pl.pallas_call(
        kernel,
        out_shape=[jax.ShapeDtypeStruct((width,), jnp.float32)] * 2,
        in_specs=[pl.BlockSpec(memory_space=pl.ANY)] * 7,
        out_specs=[vmem] * 2,
        scratch_shapes=[pltpu.VMEM(value.shape, value.dtype) for value in arguments]
        + [
            pltpu.SemaphoreType.DMA((7,)),
            pltpu.VMEM((points, depth), jnp.bfloat16),
            pltpu.VMEM((points, depth), jnp.bfloat16),
            pltpu.VMEM((4 * 8, 8 * depth), jnp.bfloat16),
            pltpu.VMEM((far_part, lanes), jnp.float32),
            pltpu.VMEM((far_part, lanes), jnp.float32),
            pltpu.VMEM((chunks, 8, lanes), jnp.float32),
            pltpu.VMEM((chunks, 8, lanes), jnp.float32),
            pltpu.VMEM((group, 2, width), jnp.float32),
            pltpu.VMEM((group, 2, width), jnp.float32),
            pltpu.VMEM((group, width), jnp.float32),
            pltpu.VMEM((group, 2, width), jnp.float32),
            pltpu.VMEM((group, 2, width), jnp.float32),
        ]
        + [pltpu.SemaphoreType.DMA((count,)) for count in (17, 17, 25, 25)]
        + [pltpu.SemaphoreType.DMA((group,))] * 6,
        compiler_params=pltpu.CompilerParams(
            collective_id=0, has_side_effects=True, vmem_limit_bytes=56 * 1024 * 1024
        ),
        name="sweep",
    )(*arguments)


def solution(mesh):
    column = P(None, ("blk", "grp"))
    flat = P(("blk", "grp"))
    return jax.shard_map(
        local,
        mesh=mesh,
        in_specs=(column, column, flat, column, column, flat, flat),
        out_specs=(flat, flat),
        check_vma=False,
    )
```

```python
import math

import jax
import jax.numpy as jnp
from jax import lax
from jax.experimental import pallas as pl
from jax.experimental.pallas import tpu as pltpu
from jax.sharding import PartitionSpec as P

epsilon = 0.25
width = 192
depth = 128
features, factors = 64, 34
offset_lane = features + factors
dual_lane = offset_lane + 3
group = 16
lanes = 768
per_chunk = lanes // width
chunks = group * width // lanes
near_rows = 7 * width
far_rows = 9 * width
near_part, far_part, even_part = near_rows // 4, far_rows // 4, group * width // 8
part_rows = width // 2
lowest = -1e30
MESH = pl.DeviceIdType.MESH


def dot_first(left, right):
    return lax.dot_general(
        left, right, (((0,), (0,)), ((), ())), preferred_element_type=jnp.float32
    )


def dot_last(left, right):
    return lax.dot_general(
        left, right, (((1,), (1,)), ((), ())), preferred_element_type=jnp.float32
    )


def placing(count, first_lane, scale):
    source = lax.broadcasted_iota(jnp.int32, (count, depth), 0)
    lane = lax.broadcasted_iota(jnp.int32, (count, depth), 1)
    return jnp.where(lane == source + first_lane, scale, 0.0).astype(jnp.bfloat16)


def pieces(row):
    high = row.astype(jnp.bfloat16).astype(jnp.float32)
    rest = row - high
    middle = rest.astype(jnp.bfloat16).astype(jnp.float32)
    low = rest - middle
    at = lax.broadcasted_iota(jnp.int32, (16, row.shape[1]), 0)
    stacked = jnp.where(at == 0, high, jnp.where(at == 1, middle, jnp.where(at == 2, low, 0.0)))
    return stacked.astype(jnp.bfloat16)


def lane_between(first, last):
    lane = lax.broadcasted_iota(jnp.int32, (width, depth), 1)
    return (lane >= first) & (lane < last)


def norms(feat):
    values = feat.astype(jnp.float32)
    return jnp.sum(values * values, axis=0, keepdims=True) * (1.0 / (features * epsilon))


def rem(value, by):
    return value % by if isinstance(value, int) else lax.rem(value, jnp.int32(by))


def div(value, by):
    return value // by if isinstance(value, int) else lax.div(value, jnp.int32(by))


def z_shift(pair):
    return jnp.where(rem(pair, 2) == 1, div(pair + 1, 2), rem(8 - div(pair, 2), 8))


def z_shift_of(pair):
    return (pair + 1) // 2 if pair % 2 else (8 - pair // 2) % 8


def shift(place):
    return place + div(place, 2) * (5 - 2 * place)


def slot_of(i, j):
    if j == 0:
        return i
    return 3 + j if i == 0 else 7 + 3 * (j - 1) + i - 1


def lines_of(slot):
    i = jnp.where(slot < 4, slot, jnp.where(slot < 7, 0, 1 + rem(slot + 2, 3)))
    j = jnp.where(slot < 4, 0, jnp.where(slot < 7, slot - 3, div(slot - 4, 3)))
    return i, j


def kernel(
    spot_feat_in, spot_fac_in, spot_mass_in, cell_feat_in, cell_fac_in, cell_mass_in, cell_pot_in,
    out,
    spot_feat, spot_fac, spot_mass, cell_feat, cell_fac, cell_mass, cell_pot, input_sem,
    spots, cells, spread, tile_a, tile_b, highest, total,
    part_1, out_1, dual, part_2, out_2,
    spot_send, spot_recv, cell_send, cell_recv,
    part_1_send, part_1_recv, dual_send, dual_recv, part_2_send, part_2_recv,
):
    blk, grp = lax.axis_index("blk"), lax.axis_index("grp")
    my_x, my_y = div(blk, 4) * 2 + div(grp, 16), rem(blk, 4)
    my_z, my_core = div(rem(grp, 16), 2), rem(grp, 2)
    same_x = grp - rem(grp, 16)

    def along_q(shift, other):
        return (blk, same_x + rem(my_z + shift, 8) * 2 + rem(my_core + other, 2))

    def along_p(dx, dy):
        x, y = rem(my_x + dx, 4), rem(my_y + dy, 4)
        return (div(x, 2) * 4 + y, rem(x, 2) * 16 + rem(grp, 16))

    barrier = pltpu.get_barrier_semaphore()
    line = (1, 2, 3)
    partners = (
        [along_q(0, 1)]
        + [along_q(z_shift_of(pair), 0) for pair in range(1, 5)]
        + [along_p(shift(i), 0) for i in line]
        + [along_p(0, shift(j)) for j in line]
    )
    for partner in partners:
        pl.semaphore_signal(barrier, inc=1, device_id=partner, device_id_type=MESH)
    loads = [
        pltpu.make_async_copy(source, target, input_sem.at[at])
        for at, (source, target) in enumerate((
            (cell_feat_in, cell_feat), (cell_fac_in, cell_fac), (cell_pot_in, cell_pot),
            (spot_feat_in, spot_feat), (spot_fac_in, spot_fac),
            (spot_mass_in, spot_mass), (cell_mass_in, cell_mass),
        ))
    ]
    for load in loads:
        load.start()

    for load in loads:
        load.wait()

    own_spots = (
        dot_first(spot_feat[...], placing(features, 0, 0.125))
        + dot_first(spot_fac[...], placing(factors, features, -4.0))
    )
    own_spots = jnp.where(lane_between(offset_lane, offset_lane + 3), 1.0, own_spots)
    spots[0:width, :] = own_spots.astype(jnp.bfloat16)
    cell_norm = norms(cell_feat[...])
    potential = cell_pot[...].reshape(1, width) * (1.0 / epsilon)
    own_cells = (
        dot_first(cell_feat[...], placing(features, 0, 1.0))
        + dot_first(cell_fac[...], placing(factors, features, 1.0))
        + dot_first(pieces(potential - cell_norm), placing(16, offset_lane, 1.0))
    )
    own_cells = jnp.where(lane_between(dual_lane, dual_lane + 3), 1.0, own_cells)
    cells[0:width, :] = own_cells.astype(jnp.bfloat16)

    pl.semaphore_wait(barrier, len(partners))

    def clear():
        highest[...] = jnp.full(highest.shape, lowest, jnp.float32)
        total[...] = jnp.zeros(total.shape, jnp.float32)

    def spot_copy(pair, source=0, first=0, count=width, flight=None):
        target = z_shift_of(pair) - z_shift_of(source)
        at = 2 * pair if flight is None else flight
        return pltpu.make_async_remote_copy(
            src_ref=spots.at[pl.ds(2 * source * width + first, count), :],
            dst_ref=spots.at[pl.ds(2 * pair * width + first, count), :],
            send_sem=spot_send.at[at],
            recv_sem=spot_recv.at[at],
            device_id=along_q((target + 8) % 8, 0),
            device_id_type=MESH,
        )

    def spot_pass(pair):
        return pltpu.make_async_remote_copy(
            src_ref=spots.at[pl.ds(2 * pair * width, width), :],
            dst_ref=spots.at[pl.ds((2 * pair + 1) * width, width), :],
            send_sem=spot_send.at[2 * pair + 1],
            recv_sem=spot_recv.at[2 * pair + 1],
            device_id=along_q(0, 1),
            device_id_type=MESH,
        )

    def cell_copy(i, j):
        slot = slot_of(i, j)
        return pltpu.make_async_remote_copy(
            src_ref=cells.at[pl.ds(0, width), :],
            dst_ref=cells.at[pl.ds(slot * width, width), :],
            send_sem=cell_send.at[slot],
            recv_sem=cell_recv.at[slot],
            device_id=along_p(shift(i), shift(j)),
            device_id_type=MESH,
        )

    def cell_turn(i, j, along_y):
        source, first = (slot_of(i, 0), 0) if along_y else (slot_of(0, j), part_rows)
        at = slot_of(i, j) + (0 if along_y else 9)
        return pltpu.make_async_remote_copy(
            src_ref=cells.at[pl.ds(source * width + first, part_rows), :],
            dst_ref=cells.at[pl.ds(slot_of(i, j) * width + first, part_rows), :],
            send_sem=cell_send.at[at],
            recv_sem=cell_recv.at[at],
            device_id=along_p(0, shift(j)) if along_y else along_p(shift(i), 0),
            device_id_type=MESH,
        )

    spot_direct = [spot_copy(pair) for pair in (3, 4, 1, 2)]
    spot_further = [
        spot_copy(5, 3),
        spot_copy(6, 4),
        spot_copy(7, 3, 0, part_rows),
        spot_copy(7, 4, part_rows, part_rows, 16),
    ]
    cell_direct = [cell_copy(0, j) for j in line] + [cell_copy(i, 0) for i in line]
    cell_turns = [
        cell_turn(i, j, along_y) for i in line for j in line for along_y in (True, False)
    ]
    passes = [spot_pass(pair) for pair in range(8)]
    passes[0].start()
    for spot_step, cell_step in zip(spot_direct, ((2, 5), (0, 3), (1,), (4,))):
        spot_step.start()
        for at in cell_step:
            cell_direct[at].start()
    source = lax.broadcasted_iota(jnp.int32, spread.shape, 0)
    target = lax.broadcasted_iota(jnp.int32, spread.shape, 1)
    lane, kind = target % depth, source // 8
    value = jnp.where(
        lane == dual_lane + kind,
        jnp.where(kind < 3, 1.0, 0.0),
        jnp.where((kind == 3) & (lane >= offset_lane) & (lane < dual_lane), -1.0, 0.0),
    )
    spread[...] = jnp.where(target // depth == source % 8, value, 0.0).astype(jnp.bfloat16)

    clear()
    for i in line:
        cell_copy(i, 0).wait_recv()
        for j in line:
            cell_turn(i, j, True).start()
        cell_copy(0, i).wait_recv()
        for j in line:
            cell_turn(j, i, False).start()
    for pair in (1, 2):
        spot_copy(pair).wait_recv()
        passes[pair].start()
    for pair in (3, 4):
        spot_copy(pair).wait_recv()
    for step in spot_further:
        step.start()
    for pair in (3, 4):
        passes[pair].start()
    passes[0].wait_recv()

    def further():
        for step in spot_further:
            step.wait_recv()
        for pair in (5, 6, 7):
            passes[pair].start()
        for step in cell_turns:
            step.wait_recv()

    def sent():
        for step in spot_direct + spot_further + cell_direct + cell_turns + passes:
            step.wait_send()

    def fill(by_row, first, count, by_lane, chunk, tile):
        right = by_lane[pl.ds(pl.multiple_of(chunk * lanes, lanes), lanes), :]
        scores = dot_last(by_row[pl.ds(first, count), :], right)
        tile[0:count, :] = scores
        return jnp.max(scores.reshape(count // 8, 8, lanes), axis=0)

    def absorb(chunk, count, tile, newest):
        before = highest[chunk]
        after = jnp.maximum(before, newest)
        highest[chunk] = after
        scores = tile[0:count, :].reshape(count // 8, 8, lanes)
        total[chunk] = total[chunk] * jnp.exp(before - after) + jnp.sum(
            jnp.exp(scores - after[None]), axis=0
        )

    def through(jobs, pending):
        for job in jobs:
            by_row, first, count, by_lane, chunk = job
            tile = tile_a if pending is None else pending[3]
            newest = fill(by_row, first, count, by_lane, chunk, tile)
            if pending is not None:
                absorb(*pending[:2], pending[2], pending[4])
            pending = (chunk, count, tile, tile_b if tile is tile_a else tile_a, newest)
        return pending

    def close(chunk, finish):
        top = jnp.max(highest[chunk], axis=0, keepdims=True)
        sums = jnp.sum(total[chunk] * jnp.exp(highest[chunk] - top), axis=0, keepdims=True)
        finish(chunk, top, sums)

    def store_pair(out, slot, top, sums, at):
        out[slot, 0:1, :] = top[:, at * width:(at + 1) * width]
        out[slot, 1:2, :] = sums[:, at * width:(at + 1) * width]

    def combine(part):
        top = part[0, 0:1, 0:width]
        for slot in range(1, group):
            top = jnp.maximum(top, part[slot, 0:1, 0:width])
        sums = jnp.zeros_like(top)
        for slot in range(group):
            sums += part[slot, 1:2, 0:width] * jnp.exp(part[slot, 0:1, 0:width] - top)
        return top + jnp.log(sums)

    def part_1_copy(slot, target):
        return pltpu.make_async_remote_copy(
            src_ref=out_1.at[slot],
            dst_ref=part_1.at[slot],
            send_sem=part_1_send.at[slot],
            recv_sem=part_1_recv.at[slot],
            device_id=target,
            device_id_type=MESH,
        )

    def finish_1(chunk, top, sums):
        last = isinstance(chunk, int)
        if last:
            store_pair(part_1, 0, top, sums, 0)
        for at in range(last, per_chunk):
            slot = per_chunk * chunk + at
            store_pair(out_1, slot, top, sums, at)
            back = rem(8 - z_shift(div(slot, 2)), 8)
            part_1_copy(slot, along_q(back, at % 2)).start()

    def near_jobs(chunk):
        return [(cells, part * near_part, near_part, spots, chunk) for part in range(4)]

    def far_jobs(chunk):
        return [(cells, near_rows + part * far_part, far_part, spots, chunk) for part in range(4)]

    def rest(pending):
        return pending[0], pending[1], pending[2], pending[4]

    passes[1].wait_recv()
    pending = through(near_jobs(0), None)
    for pair in (2, 3):
        passes[pair].wait_recv()
    pending = through(near_jobs(1), pending)
    further()
    passes[4].wait_recv()
    pending = through(far_jobs(1), pending)
    for pair in (5, 6, 7):
        passes[pair].wait_recv()

    def last_tiles(step, newest):
        chunk = 3 - step
        before = jnp.where(step == 0, 1, chunk + 1)
        held = (before, far_part, tile_b, tile_a, newest)
        held = through(near_jobs(chunk)[:1], held)
        close(before, finish_1)
        held = through(near_jobs(chunk)[1:] + far_jobs(chunk), held)
        return held[4]

    newest = lax.fori_loop(0, 2, last_tiles, pending[4])
    pending = through(far_jobs(0)[:1], (2, far_part, tile_b, tile_a, newest))
    close(jnp.int32(2), finish_1)
    pending = through(far_jobs(0)[1:], pending)
    absorb(*rest(pending))
    close(0, finish_1)

    sent()
    for slot in range(1, group):
        part_1_copy(slot, along_q((8 - z_shift_of(slot // 2)) % 8, slot % 2)).wait()
    log_sum = combine(part_1)
    mass = spot_mass[...].reshape(1, width)
    log_count = math.log(256 * width)
    term = mass - log_sum + log_count
    out[0:1, :] = epsilon * (term + norms(spot_feat[...]))
    dual[0:1, :] = term

    def dual_copy(slot):
        return pltpu.make_async_remote_copy(
            src_ref=dual.at[pl.ds(0, 1), :],
            dst_ref=dual.at[pl.ds(slot, 1), :],
            send_sem=dual_send.at[slot],
            recv_sem=dual_recv.at[slot],
            device_id=along_q(z_shift_of(slot // 2), slot % 2),
            device_id_type=MESH,
        )

    for slot in range(group - 1, 0, -1):
        dual_copy(slot).start()

    def take_terms(part):
        values = dual[8 * part:8 * part + 8, :]
        high = values.astype(jnp.bfloat16).astype(jnp.float32)
        middle = (values - high).astype(jnp.bfloat16).astype(jnp.float32)
        low = values - high - middle
        stacked = jnp.concatenate([high, middle, low, jnp.ones_like(low)], axis=0)
        moved = dot_first(stacked.astype(jnp.bfloat16), spread[...]).astype(jnp.bfloat16)
        for at in range(8):
            own = slice((8 * part + at) * width, (8 * part + at + 1) * width)
            spots[own, :] = spots[own, :] + moved[:, at * depth:(at + 1) * depth]

    for slot in range(1, 8):
        dual_copy(slot).wait()
    take_terms(0)

    def part_2_copy(slot, target):
        return pltpu.make_async_remote_copy(
            src_ref=out_2.at[slot],
            dst_ref=part_2.at[slot],
            send_sem=part_2_send.at[slot],
            recv_sem=part_2_recv.at[slot],
            device_id=target,
            device_id_type=MESH,
        )

    def owner(slot):
        i, j = lines_of(slot)
        return along_p(4 - shift(i), 4 - shift(j))

    def finish_2(chunk, top, sums):
        last = isinstance(chunk, int)
        if last:
            store_pair(part_2, 0, top, sums, 0)
        for at in range(last, per_chunk):
            slot = per_chunk * chunk + at
            store_pair(out_2, slot, top, sums, at)
            part_2_copy(slot, owner(slot)).start()

    def even_jobs(chunk):
        return [(spots, part * even_part, even_part, cells, chunk) for part in range(8)]

    clear()
    top_chunk = chunks - 1
    pending = through(even_jobs(top_chunk)[:4], None)
    for slot in range(8, group):
        dual_copy(slot).wait()
    take_terms(1)
    pending = through(even_jobs(top_chunk)[4:], pending)

    def next_chunk(step, newest):
        chunk = chunks - 2 - step
        held = (chunk + 1, even_part, tile_b, tile_a, newest)
        held = through(even_jobs(chunk)[:1], held)
        close(chunk + 1, finish_2)
        return through(even_jobs(chunk)[1:], held)[4]

    newest = lax.fori_loop(0, chunks - 1, next_chunk, pending[4])
    absorb(0, even_part, tile_b, newest)
    close(0, finish_2)
    for slot in range(1, group):
        part_2_copy(slot, owner(slot)).wait()
    log_sum = combine(part_2)
    mass = cell_mass[...].reshape(1, width)
    out[1:2, :] = epsilon * (mass - log_sum + norms(cell_feat[...]) + log_count)


def local(*arguments):
    vmem = pl.BlockSpec(memory_space=pltpu.VMEM)
    points = group * width
    both = pl.pallas_call(
        kernel,
        out_shape=jax.ShapeDtypeStruct((2, width), jnp.float32),
        in_specs=[pl.BlockSpec(memory_space=pl.ANY)] * 7,
        out_specs=vmem,
        scratch_shapes=[pltpu.VMEM(value.shape, value.dtype) for value in arguments]
        + [
            pltpu.SemaphoreType.DMA((7,)),
            pltpu.VMEM((points, depth), jnp.bfloat16),
            pltpu.VMEM((points, depth), jnp.bfloat16),
            pltpu.VMEM((4 * 8, 8 * depth), jnp.bfloat16),
            pltpu.VMEM((far_part, lanes), jnp.float32),
            pltpu.VMEM((far_part, lanes), jnp.float32),
            pltpu.VMEM((chunks, 8, lanes), jnp.float32),
            pltpu.VMEM((chunks, 8, lanes), jnp.float32),
            pltpu.VMEM((group, 2, width), jnp.float32),
            pltpu.VMEM((group, 2, width), jnp.float32),
            pltpu.VMEM((group, width), jnp.float32),
            pltpu.VMEM((group, 2, width), jnp.float32),
            pltpu.VMEM((group, 2, width), jnp.float32),
        ]
        + [pltpu.SemaphoreType.DMA((count,)) for count in (17, 17, 25, 25)]
        + [pltpu.SemaphoreType.DMA((group,))] * 6,
        compiler_params=pltpu.CompilerParams(
            collective_id=0, has_side_effects=True, vmem_limit_bytes=56 * 1024 * 1024
        ),
        name="sweep",
    )(*arguments)
    return both[0], both[1]


def solution(mesh):
    column = P(None, ("blk", "grp"))
    flat = P(("blk", "grp"))
    return jax.shard_map(
        local,
        mesh=mesh,
        in_specs=(column, column, flat, column, column, flat, flat),
        out_specs=(flat, flat),
        check_vma=False,
    )
```

```python
import math

import jax
import jax.numpy as jnp
from jax import lax
from jax.experimental import pallas as pl
from jax.experimental.pallas import tpu as pltpu
from jax.sharding import PartitionSpec as P

epsilon = 0.25
width = 192
depth = 128
features, factors = 64, 34
offset_lane = features + factors
dual_lane = offset_lane + 3
group = 16
lanes = 768
per_chunk = lanes // width
chunks = group * width // lanes
near_rows = 7 * width
far_rows = 9 * width
near_part, far_part, even_part = near_rows // 6, far_rows // 6, group * width // 12
part_rows = width // 2
lowest = -1e30
MESH = pl.DeviceIdType.MESH


def dot_first(left, right):
    return lax.dot_general(
        left, right, (((0,), (0,)), ((), ())), preferred_element_type=jnp.float32
    )


def dot_last(left, right):
    return lax.dot_general(
        left, right, (((1,), (1,)), ((), ())), preferred_element_type=jnp.float32
    )


def placing(count, first_lane, scale):
    source = lax.broadcasted_iota(jnp.int32, (count, depth), 0)
    lane = lax.broadcasted_iota(jnp.int32, (count, depth), 1)
    return jnp.where(lane == source + first_lane, scale, 0.0).astype(jnp.bfloat16)


def pieces(row):
    high = row.astype(jnp.bfloat16).astype(jnp.float32)
    rest = row - high
    middle = rest.astype(jnp.bfloat16).astype(jnp.float32)
    low = rest - middle
    at = lax.broadcasted_iota(jnp.int32, (16, row.shape[1]), 0)
    stacked = jnp.where(at == 0, high, jnp.where(at == 1, middle, jnp.where(at == 2, low, 0.0)))
    return stacked.astype(jnp.bfloat16)


def lane_between(first, last):
    lane = lax.broadcasted_iota(jnp.int32, (width, depth), 1)
    return (lane >= first) & (lane < last)


def norms(feat):
    values = feat.astype(jnp.float32)
    return jnp.sum(values * values, axis=0, keepdims=True) * (1.0 / (features * epsilon))


def rem(value, by):
    return value % by if isinstance(value, int) else lax.rem(value, jnp.int32(by))


def div(value, by):
    return value // by if isinstance(value, int) else lax.div(value, jnp.int32(by))


def z_shift(pair):
    return jnp.where(rem(pair, 2) == 1, div(pair + 1, 2), rem(8 - div(pair, 2), 8))


def z_shift_of(pair):
    return (pair + 1) // 2 if pair % 2 else (8 - pair // 2) % 8


def shift(place):
    return place + div(place, 2) * (5 - 2 * place)


def slot_of(i, j):
    if j == 0:
        return i
    return 3 + j if i == 0 else 7 + 3 * (j - 1) + i - 1


def lines_of(slot):
    i = jnp.where(slot < 4, slot, jnp.where(slot < 7, 0, 1 + rem(slot + 2, 3)))
    j = jnp.where(slot < 4, 0, jnp.where(slot < 7, slot - 3, div(slot - 4, 3)))
    return i, j


def kernel(
    spot_feat_in, spot_fac_in, spot_mass_in, cell_feat_in, cell_fac_in, cell_mass_in, cell_pot_in,
    out,
    spot_feat, spot_fac, spot_mass, cell_feat, cell_fac, cell_mass, cell_pot, input_sem,
    spots, cells, spread, tile_a, tile_b, highest, total,
    part_1, out_1, dual, part_2, out_2,
    spot_send, spot_recv, cell_send, cell_recv,
    part_1_send, part_1_recv, dual_send, dual_recv, part_2_send, part_2_recv,
):
    blk, grp = lax.axis_index("blk"), lax.axis_index("grp")
    my_x, my_y = div(blk, 4) * 2 + div(grp, 16), rem(blk, 4)
    my_z, my_core = div(rem(grp, 16), 2), rem(grp, 2)
    same_x = grp - rem(grp, 16)

    def along_q(shift, other):
        return (blk, same_x + rem(my_z + shift, 8) * 2 + rem(my_core + other, 2))

    def along_p(dx, dy):
        x, y = rem(my_x + dx, 4), rem(my_y + dy, 4)
        return (div(x, 2) * 4 + y, rem(x, 2) * 16 + rem(grp, 16))

    barrier = pltpu.get_barrier_semaphore()
    line = (1, 2, 3)
    partners = (
        [along_q(0, 1)]
        + [along_q(z_shift_of(pair), 0) for pair in range(1, 5)]
        + [along_p(shift(i), 0) for i in line]
        + [along_p(0, shift(j)) for j in line]
    )
    for partner in partners:
        pl.semaphore_signal(barrier, inc=1, device_id=partner, device_id_type=MESH)
    loads = [
        pltpu.make_async_copy(source, target, input_sem.at[at])
        for at, (source, target) in enumerate((
            (cell_feat_in, cell_feat), (cell_fac_in, cell_fac), (cell_pot_in, cell_pot),
            (spot_feat_in, spot_feat), (spot_fac_in, spot_fac),
            (spot_mass_in, spot_mass), (cell_mass_in, cell_mass),
        ))
    ]
    for load in loads:
        load.start()

    for load in loads:
        load.wait()

    own_spots = (
        dot_first(spot_feat[...], placing(features, 0, 0.125))
        + dot_first(spot_fac[...], placing(factors, features, -4.0))
    )
    own_spots = jnp.where(lane_between(offset_lane, offset_lane + 3), 1.0, own_spots)
    spots[0:width, :] = own_spots.astype(jnp.bfloat16)
    cell_norm = norms(cell_feat[...])
    potential = cell_pot[...].reshape(1, width) * (1.0 / epsilon)
    own_cells = (
        dot_first(cell_feat[...], placing(features, 0, 1.0))
        + dot_first(cell_fac[...], placing(factors, features, 1.0))
        + dot_first(pieces(potential - cell_norm), placing(16, offset_lane, 1.0))
    )
    own_cells = jnp.where(lane_between(dual_lane, dual_lane + 3), 1.0, own_cells)
    cells[0:width, :] = own_cells.astype(jnp.bfloat16)

    pl.semaphore_wait(barrier, len(partners))

    def clear():
        highest[...] = jnp.full(highest.shape, lowest, jnp.float32)
        total[...] = jnp.zeros(total.shape, jnp.float32)

    def spot_copy(pair, source=0, first=0, count=width, flight=None):
        target = z_shift_of(pair) - z_shift_of(source)
        at = 2 * pair if flight is None else flight
        return pltpu.make_async_remote_copy(
            src_ref=spots.at[pl.ds(2 * source * width + first, count), :],
            dst_ref=spots.at[pl.ds(2 * pair * width + first, count), :],
            send_sem=spot_send.at[at],
            recv_sem=spot_recv.at[at],
            device_id=along_q((target + 8) % 8, 0),
            device_id_type=MESH,
        )

    def spot_pass(pair):
        return pltpu.make_async_remote_copy(
            src_ref=spots.at[pl.ds(2 * pair * width, width), :],
            dst_ref=spots.at[pl.ds((2 * pair + 1) * width, width), :],
            send_sem=spot_send.at[2 * pair + 1],
            recv_sem=spot_recv.at[2 * pair + 1],
            device_id=along_q(0, 1),
            device_id_type=MESH,
        )

    def cell_copy(i, j):
        slot = slot_of(i, j)
        return pltpu.make_async_remote_copy(
            src_ref=cells.at[pl.ds(0, width), :],
            dst_ref=cells.at[pl.ds(slot * width, width), :],
            send_sem=cell_send.at[slot],
            recv_sem=cell_recv.at[slot],
            device_id=along_p(shift(i), shift(j)),
            device_id_type=MESH,
        )

    def cell_turn(i, j, along_y):
        source, first = (slot_of(i, 0), 0) if along_y else (slot_of(0, j), part_rows)
        at = slot_of(i, j) + (0 if along_y else 9)
        return pltpu.make_async_remote_copy(
            src_ref=cells.at[pl.ds(source * width + first, part_rows), :],
            dst_ref=cells.at[pl.ds(slot_of(i, j) * width + first, part_rows), :],
            send_sem=cell_send.at[at],
            recv_sem=cell_recv.at[at],
            device_id=along_p(0, shift(j)) if along_y else along_p(shift(i), 0),
            device_id_type=MESH,
        )

    spot_direct = [spot_copy(pair) for pair in (3, 4, 1, 2)]
    spot_further = [
        spot_copy(5, 3),
        spot_copy(6, 4),
        spot_copy(7, 3, 0, part_rows),
        spot_copy(7, 4, part_rows, part_rows, 16),
    ]
    cell_direct = [cell_copy(0, j) for j in line] + [cell_copy(i, 0) for i in line]
    cell_turns = [
        cell_turn(i, j, along_y) for i in line for j in line for along_y in (True, False)
    ]
    passes = [spot_pass(pair) for pair in range(8)]
    passes[0].start()
    for spot_step, cell_step in zip(spot_direct, ((2, 5), (0, 3), (1,), (4,))):
        spot_step.start()
        for at in cell_step:
            cell_direct[at].start()
    source = lax.broadcasted_iota(jnp.int32, spread.shape, 0)
    target = lax.broadcasted_iota(jnp.int32, spread.shape, 1)
    lane, kind = target % depth, source // 8
    value = jnp.where(
        lane == dual_lane + kind,
        jnp.where(kind < 3, 1.0, 0.0),
        jnp.where((kind == 3) & (lane >= offset_lane) & (lane < dual_lane), -1.0, 0.0),
    )
    spread[...] = jnp.where(target // depth == source % 8, value, 0.0).astype(jnp.bfloat16)

    clear()
    for i in line:
        cell_copy(i, 0).wait_recv()
        for j in line:
            cell_turn(i, j, True).start()
        cell_copy(0, i).wait_recv()
        for j in line:
            cell_turn(j, i, False).start()
    for pair in (1, 2):
        spot_copy(pair).wait_recv()
        passes[pair].start()
    for pair in (3, 4):
        spot_copy(pair).wait_recv()
    for step in spot_further:
        step.start()
    for pair in (3, 4):
        passes[pair].start()
    passes[0].wait_recv()

    def further():
        for step in spot_further:
            step.wait_recv()
        for pair in (5, 6, 7):
            passes[pair].start()
        for step in cell_turns:
            step.wait_recv()

    def sent():
        for step in spot_direct + spot_further + cell_direct + cell_turns + passes:
            step.wait_send()

    def fill(by_row, first, count, by_lane, chunk, tile):
        right = by_lane[pl.ds(pl.multiple_of(chunk * lanes, lanes), lanes), :]
        scores = dot_last(by_row[pl.ds(first, count), :], right)
        tile[0:count, :] = scores
        return jnp.max(scores.reshape(count // 8, 8, lanes), axis=0)

    def absorb(chunk, count, tile, newest):
        before = highest[chunk]
        after = jnp.maximum(before, newest)
        highest[chunk] = after
        scores = tile[0:count, :].reshape(count // 8, 8, lanes)
        total[chunk] = total[chunk] * jnp.exp(before - after) + jnp.sum(
            jnp.exp(scores - after[None]), axis=0
        )

    def through(jobs, pending):
        for job in jobs:
            by_row, first, count, by_lane, chunk = job
            tile = tile_a if pending is None else pending[3]
            newest = fill(by_row, first, count, by_lane, chunk, tile)
            if pending is not None:
                absorb(*pending[:2], pending[2], pending[4])
            pending = (chunk, count, tile, tile_b if tile is tile_a else tile_a, newest)
        return pending

    def close(chunk, finish):
        top = jnp.max(highest[chunk], axis=0, keepdims=True)
        sums = jnp.sum(total[chunk] * jnp.exp(highest[chunk] - top), axis=0, keepdims=True)
        finish(chunk, top, sums)

    def store_pair(out, slot, top, sums, at):
        out[slot, 0:1, :] = top[:, at * width:(at + 1) * width]
        out[slot, 1:2, :] = sums[:, at * width:(at + 1) * width]

    def combine(part):
        top = part[0, 0:1, 0:width]
        for slot in range(1, group):
            top = jnp.maximum(top, part[slot, 0:1, 0:width])
        sums = jnp.zeros_like(top)
        for slot in range(group):
            sums += part[slot, 1:2, 0:width] * jnp.exp(part[slot, 0:1, 0:width] - top)
        return top + jnp.log(sums)

    def part_1_copy(slot, target):
        return pltpu.make_async_remote_copy(
            src_ref=out_1.at[slot],
            dst_ref=part_1.at[slot],
            send_sem=part_1_send.at[slot],
            recv_sem=part_1_recv.at[slot],
            device_id=target,
            device_id_type=MESH,
        )

    def finish_1(chunk, top, sums):
        last = isinstance(chunk, int)
        if last:
            store_pair(part_1, 0, top, sums, 0)
        for at in range(last, per_chunk):
            slot = per_chunk * chunk + at
            store_pair(out_1, slot, top, sums, at)
            back = rem(8 - z_shift(div(slot, 2)), 8)
            part_1_copy(slot, along_q(back, at % 2)).start()

    def near_jobs(chunk):
        return [(cells, part * near_part, near_part, spots, chunk) for part in range(6)]

    def far_jobs(chunk):
        return [(cells, near_rows + part * far_part, far_part, spots, chunk) for part in range(6)]

    def rest(pending):
        return pending[0], pending[1], pending[2], pending[4]

    passes[1].wait_recv()
    pending = through(near_jobs(0), None)
    for pair in (2, 3):
        passes[pair].wait_recv()
    pending = through(near_jobs(1), pending)
    further()
    passes[4].wait_recv()
    pending = through(far_jobs(1), pending)
    for pair in (5, 6, 7):
        passes[pair].wait_recv()

    def last_tiles(step, newest):
        chunk = 3 - step
        before = jnp.where(step == 0, 1, chunk + 1)
        held = (before, far_part, tile_b, tile_a, newest)
        held = through(near_jobs(chunk)[:1], held)
        close(before, finish_1)
        held = through(near_jobs(chunk)[1:] + far_jobs(chunk), held)
        return held[4]

    newest = lax.fori_loop(0, 2, last_tiles, pending[4])
    pending = through(far_jobs(0)[:1], (2, far_part, tile_b, tile_a, newest))
    close(jnp.int32(2), finish_1)
    pending = through(far_jobs(0)[1:], pending)
    absorb(*rest(pending))
    close(0, finish_1)

    sent()
    for slot in range(1, group):
        part_1_copy(slot, along_q((8 - z_shift_of(slot // 2)) % 8, slot % 2)).wait()
    log_sum = combine(part_1)
    mass = spot_mass[...].reshape(1, width)
    log_count = math.log(256 * width)
    term = mass - log_sum + log_count
    out[0:1, :] = epsilon * (term + norms(spot_feat[...]))
    dual[0:1, :] = term

    def dual_copy(slot):
        return pltpu.make_async_remote_copy(
            src_ref=dual.at[pl.ds(0, 1), :],
            dst_ref=dual.at[pl.ds(slot, 1), :],
            send_sem=dual_send.at[slot],
            recv_sem=dual_recv.at[slot],
            device_id=along_q(z_shift_of(slot // 2), slot % 2),
            device_id_type=MESH,
        )

    for slot in range(group - 1, 0, -1):
        dual_copy(slot).start()

    def take_terms(part):
        values = dual[8 * part:8 * part + 8, :]
        high = values.astype(jnp.bfloat16).astype(jnp.float32)
        middle = (values - high).astype(jnp.bfloat16).astype(jnp.float32)
        low = values - high - middle
        stacked = jnp.concatenate([high, middle, low, jnp.ones_like(low)], axis=0)
        moved = dot_first(stacked.astype(jnp.bfloat16), spread[...]).astype(jnp.bfloat16)
        for at in range(8):
            own = slice((8 * part + at) * width, (8 * part + at + 1) * width)
            spots[own, :] = spots[own, :] + moved[:, at * depth:(at + 1) * depth]

    for slot in range(1, 8):
        dual_copy(slot).wait()
    take_terms(0)

    def part_2_copy(slot, target):
        return pltpu.make_async_remote_copy(
            src_ref=out_2.at[slot],
            dst_ref=part_2.at[slot],
            send_sem=part_2_send.at[slot],
            recv_sem=part_2_recv.at[slot],
            device_id=target,
            device_id_type=MESH,
        )

    def owner(slot):
        i, j = lines_of(slot)
        return along_p(4 - shift(i), 4 - shift(j))

    def finish_2(chunk, top, sums):
        last = isinstance(chunk, int)
        if last:
            store_pair(part_2, 0, top, sums, 0)
        for at in range(last, per_chunk):
            slot = per_chunk * chunk + at
            store_pair(out_2, slot, top, sums, at)
            part_2_copy(slot, owner(slot)).start()

    def even_jobs(chunk):
        return [(spots, part * even_part, even_part, cells, chunk) for part in range(12)]

    clear()
    top_chunk = chunks - 1
    pending = through(even_jobs(top_chunk)[:6], None)
    for slot in range(8, group):
        dual_copy(slot).wait()
    take_terms(1)
    pending = through(even_jobs(top_chunk)[6:], pending)

    def next_chunk(step, newest):
        chunk = chunks - 2 - step
        held = (chunk + 1, even_part, tile_b, tile_a, newest)
        held = through(even_jobs(chunk)[:1], held)
        close(chunk + 1, finish_2)
        return through(even_jobs(chunk)[1:], held)[4]

    newest = lax.fori_loop(0, chunks - 1, next_chunk, pending[4])
    absorb(0, even_part, tile_b, newest)
    close(0, finish_2)
    for slot in range(1, group):
        part_2_copy(slot, owner(slot)).wait()
    log_sum = combine(part_2)
    mass = cell_mass[...].reshape(1, width)
    out[1:2, :] = epsilon * (mass - log_sum + norms(cell_feat[...]) + log_count)


def local(*arguments):
    vmem = pl.BlockSpec(memory_space=pltpu.VMEM)
    points = group * width
    both = pl.pallas_call(
        kernel,
        out_shape=jax.ShapeDtypeStruct((2, width), jnp.float32),
        in_specs=[pl.BlockSpec(memory_space=pl.ANY)] * 7,
        out_specs=vmem,
        scratch_shapes=[pltpu.VMEM(value.shape, value.dtype) for value in arguments]
        + [
            pltpu.SemaphoreType.DMA((7,)),
            pltpu.VMEM((points, depth), jnp.bfloat16),
            pltpu.VMEM((points, depth), jnp.bfloat16),
            pltpu.VMEM((4 * 8, 8 * depth), jnp.bfloat16),
            pltpu.VMEM((far_part, lanes), jnp.float32),
            pltpu.VMEM((far_part, lanes), jnp.float32),
            pltpu.VMEM((chunks, 8, lanes), jnp.float32),
            pltpu.VMEM((chunks, 8, lanes), jnp.float32),
            pltpu.VMEM((group, 2, width), jnp.float32),
            pltpu.VMEM((group, 2, width), jnp.float32),
            pltpu.VMEM((group, width), jnp.float32),
            pltpu.VMEM((group, 2, width), jnp.float32),
            pltpu.VMEM((group, 2, width), jnp.float32),
        ]
        + [pltpu.SemaphoreType.DMA((count,)) for count in (17, 17, 25, 25)]
        + [pltpu.SemaphoreType.DMA((group,))] * 6,
        compiler_params=pltpu.CompilerParams(
            collective_id=0, has_side_effects=True, vmem_limit_bytes=56 * 1024 * 1024
        ),
        name="sweep",
    )(*arguments)
    return both[0], both[1]


def solution(mesh):
    column = P(None, ("blk", "grp"))
    flat = P(("blk", "grp"))
    return jax.shard_map(
        local,
        mesh=mesh,
        in_specs=(column, column, flat, column, column, flat, flat),
        out_specs=(flat, flat),
        check_vma=False,
    )
```
